128 devices in a mesh: seq: 64 (over z, x, y), head: 2 (over core).
Axes of the slice: x: 4, y: 4, z: 4, core: 2. Of those that a mesh axis runs over, the one named last changes fastest.
Arguments:
- hidden_in: bfloat16 [16384, 1024], P('seq'), may hold values from -16 to 16
- norm1_gain: float32 [1024], replicated, may hold values from 0.5 to 1.5
- in_weight: bfloat16 [1024, 3, 1024], P(None, None, 'head'), may hold values from -0.1875 to 0.1875
- conv_weight: float32 [1024, 3], P('head'), may hold values from -3.5 to 3.5
- out_weight: bfloat16 [1024, 1024], P('head'), may hold values from -0.1875 to 0.1875
- norm2_gain: float32 [1024], replicated, may hold values from 0.5 to 1.5
- gate_weight: bfloat16 [1024, 4608], P(None, 'head'), may hold values from -0.1875 to 0.1875
- up_weight: bfloat16 [1024, 4608], P(None, 'head'), may hold values from -0.1875 to 0.1875
- down_weight: bfloat16 [4608, 1024], P('head'), may hold values from -0.09375 to 0.09375
- cotangent: bfloat16 [16384, 1024], P('seq'), may hold values from -6 to 6
Outputs:
- block_out: bfloat16 [16384, 1024], P('seq')
- input_grad: bfloat16 [16384, 1024], P('seq')
- norm1_gain_grad: float32 [1024], P('seq')
- in_weight_grad: float32 [1024, 3, 1024], P('seq', None, 'head')
- conv_weight_grad: float32 [1024, 3], P(('head', 'seq'))
- out_weight_grad: float32 [1024, 1024], P(('head', 'seq'))
- norm2_gain_grad: float32 [1024], P('seq')
- gate_weight_grad: float32 [1024, 4608], P('seq', 'head')
- up_weight_grad: float32 [1024, 4608], P('seq', 'head')
- down_weight_grad: float32 [4608, 1024], P(('head', 'seq'))
The draws below stay inside these ranges and needn't reach their ends.
All inputs are finite; a program needn't handle non-finite values.
Results may differ from the reference program's by a relative error of at most 0.019.
Values may be sent and summed in bfloat16 or wider, within the bound.
A program may use at most 192 MiB of HBM per device.

```python
import jax
import jax.numpy as jnp
from jax import lax

D = 1024
FF = 4608
CONV = 3
TOKENS = 16384
SEQ_LEN = 4096
SEQS = 4


def strengthened(array, rng, source, target, shards_of, factor):
    owner, partner = [(jnp.arange(array.shape[position]) // (array.shape[position] // shards_of)).reshape([-1 if axis == position else 1 for axis in range(array.ndim)]) for position in (source, target)]
    chosen = jax.random.permutation(rng, shards_of)[partner]
    strong = (owner == chosen) | (owner == (partner + shards_of // 2) % shards_of)
    return jnp.where(strong, factor * array, array)


def level_of(own_key, dims, pieces, low, largest):
    def one(dim, blocks):
        heights = jax.random.uniform(jax.random.fold_in(jax.random.fold_in(own_key, 6), dim), (blocks,), jnp.float32, low / len(pieces), largest / len(pieces))
        return jnp.repeat(jnp.exp(heights), dims[dim] // blocks).reshape((-1,) + (1,) * (len(dims) - dim - 1))

    loudness = one(*pieces[0])
    for cut in pieces[1:]:
        loudness = loudness * one(*cut)
    return loudness


def normal_values(own_key, extent, scale, reach, split=(), held_as=jnp.bfloat16):
    level = level_of(own_key, extent, split, -0.22, 0.18) if split else 1.0
    array = jax.random.normal(own_key, extent, jnp.float32) * scale * level
    return jnp.minimum(jnp.maximum(array, -reach), reach).astype(held_as)


def heavy_noise(key, extent, spread, bound, cuts, heavy, kind=jnp.bfloat16):
    values = spread * jax.random.normal(key, extent, jnp.float32)
    if cuts:
        values = values * level_of(key, extent, cuts, -0.22, 0.18)
    return jnp.clip(strengthened(values, jax.random.fold_in(key, 3), *heavy), -bound, bound).astype(kind)


def setup_inputs(seed: int = 0) -> dict:
    key_of = jax.random.split(jax.random.key(seed), 11)
    return {
        "hidden_in": heavy_noise(key_of[0], (TOKENS, D), 1.0, 16.0, ((0, 64),), (0, 1, 64, 4.0)),
        "norm1_gain": jnp.clip(1.0 + 0.1 * jax.random.normal(key_of[1], (D,), jnp.float32), 0.5, 1.5),
        "in_weight": normal_values(key_of[2], (D, 3, D), D ** -0.5, 0.1875, ((2, 2),)),
        "conv_weight": normal_values(key_of[3], (D, CONV), CONV ** -0.5, 3.5, ((0, 2),), jnp.float32),
        "out_weight": normal_values(key_of[4], (D, D), D ** -0.5, 0.1875, ((0, 2),)),
        "norm2_gain": jnp.clip(1.0 + 0.1 * jax.random.normal(key_of[5], (D,), jnp.float32), 0.5, 1.5),
        "gate_weight": normal_values(key_of[6], (D, FF), D ** -0.5, 0.1875, ((1, 2),)),
        "up_weight": normal_values(key_of[7], (D, FF), D ** -0.5, 0.1875, ((1, 2),)),
        "down_weight": normal_values(key_of[8], (FF, D), FF ** -0.5, 0.09375, ((0, 2),)),
        "cotangent": normal_values(key_of[9], (TOKENS, D), 1.0, 6.0, ((0, 64),)),
    }


@jax.custom_vjp
def low(v):
    return lax.optimization_barrier(v.astype(jnp.bfloat16)).astype(jnp.float32)

@jax.custom_vjp
def low_back(v):
    return v

def low_keep(v):
    return (low(v), None)

def low_pass(kept, grad):
    return (grad,)

def back_keep(v):
    return (v, None)

def back_low(kept, grad):
    return (low(grad),)
low.defvjp(low_keep, low_pass)
low_back.defvjp(back_keep, back_low)
EPS = 1e-05

def matmul(left, right):
    return jnp.dot(left, right, precision=lax.Precision.HIGHEST, preferred_element_type=jnp.float32)

def rms_scale(values):
    return lax.rsqrt(lax.optimization_barrier(jnp.mean(values * values, axis=-1, keepdims=True)) + EPS)

def forward(inputs, first_gain, in_weight, conv_weight, out_weight, second_gain, gate_weight, up_weight, down_weight):
    normed = low(inputs * rms_scale(inputs) * first_gain)
    projected = low_back(matmul(normed, in_weight.reshape(D, 3 * D)))
    b_part = projected[:, :D]
    c_part = projected[:, D:2 * D]
    x_part = projected[:, 2 * D:]
    gated = low(b_part * x_part)
    padded = jnp.concatenate([jnp.zeros((2, D), jnp.float32), gated], axis=0)
    convolved = conv_weight[:, 0] * padded[:-2] + conv_weight[:, 1] * padded[1:-1] + conv_weight[:, 2] * padded[2:]
    mixed = low(c_part * convolved)
    middle = inputs + low_back(matmul(mixed, out_weight))
    normed_two = low(middle * rms_scale(middle) * second_gain)
    gate_pre = low_back(matmul(normed_two, gate_weight))
    up_pre = low_back(matmul(normed_two, up_weight))
    hidden = low(jax.nn.silu(gate_pre) * up_pre)
    return middle + low_back(matmul(hidden, down_weight))

def reference(hidden_in, norm1_gain, in_weight, conv_weight, out_weight, norm2_gain, gate_weight, up_weight, down_weight, cotangent):
    params = tuple((p.astype(jnp.float32) for p in (norm1_gain, in_weight, conv_weight, out_weight, norm2_gain, gate_weight, up_weight, down_weight)))
    inputs_all = hidden_in.astype(jnp.float32).reshape(SEQS, SEQ_LEN, D)
    cot_all = cotangent.astype(jnp.float32).reshape(SEQS, SEQ_LEN, D)

    def one_sequence(grad_totals, pair):
        inputs, cot_seq = pair
        result, pullback = jax.vjp(forward, inputs, *params)
        grads = pullback(cot_seq)
        grad_totals = tuple((a + b for a, b in zip(grad_totals, grads[1:])))
        return (grad_totals, (result, grads[0]))
    start = tuple((jnp.zeros_like(p) for p in params))
    totals, (results, input_grads) = lax.scan(one_sequence, start, (inputs_all, cot_all))
    return (results.reshape(TOKENS, D).astype(jnp.bfloat16), input_grads.reshape(TOKENS, D).astype(jnp.bfloat16), totals[0], totals[1], totals[2], totals[3], totals[4], totals[5], totals[6], totals[7])
```

```python
import functools
import jax
import jax.numpy as jnp
from jax import lax
from jax.experimental import pallas as pl
from jax.experimental.pallas import tpu as pltpu
from jax.sharding import PartitionSpec as P

EPS = 1e-05
SEQ_BASE = 4096
MESH = pl.DeviceIdType.MESH
F32 = jnp.float32
BF16 = jnp.bfloat16
NT = (((1,), (1,)), ((), ()))
N_SEMS = 170


class Place:
    def __init__(self):
        self.seq = lax.axis_index("seq")
        self.head = lax.axis_index("head")
        self.coord = {
            "z": lax.div(self.seq, 16),
            "x": lax.rem(lax.div(self.seq, 4), 4),
            "y": lax.rem(self.seq, 4),
        }

    def peer(self, axis, shift):
        moved = dict(self.coord)
        moved[axis] = lax.rem(moved[axis] + shift, 4)
        return ((moved["z"] * 4 + moved["x"]) * 4 + moved["y"], self.head)

    def sibling(self):
        return (self.seq, 1 - self.head)


class Links:
    def __init__(self, send_sem, recv_sem):
        self.send_sem = send_sem
        self.recv_sem = recv_sem
        self.used = 0
        self.open = []

    def send(self, src, dst, device):
        copy = pltpu.make_async_remote_copy(
            src_ref=src,
            dst_ref=dst,
            send_sem=self.send_sem.at[self.used],
            recv_sem=self.recv_sem.at[self.used],
            device_id=device,
            device_id_type=MESH,
        )
        self.used += 1
        copy.start()
        self.open.append(copy)
        return copy

    def close(self):
        for copy in self.open:
            copy.wait_send()


class Ring:
    def __init__(self, place, links, axis, view, first, second):
        self.place, self.links, self.axis, self.view = place, links, axis, view
        self.first, self.second = first, second
        self.me = place.coord[axis]

    def block(self, shift):
        return lax.rem(self.me + shift, 4)

    def start(self):
        right, left = self.place.peer(self.axis, 1), self.place.peer(self.axis, 3)
        send = self.links.send
        self.far = [
            send(self.view(self.block(2), 0), self.first.at[0], right),
            send(self.view(self.block(2), 1), self.first.at[1], left),
        ]
        self.near = [
            send(self.view(self.block(1), 1), self.second.at[0, 1], right),
            send(self.view(self.block(3), 0), self.second.at[1, 0], left),
        ]

    def pass_on(self):
        right, left = self.place.peer(self.axis, 1), self.place.peer(self.axis, 3)
        for half, shift, device in ((0, 1, right), (1, 3, left)):
            self.far[half].wait_recv()
            own = self.view(self.block(shift), half)
            own[...] = (own[...].astype(F32) + self.first[half].astype(F32)).astype(BF16)
            self.near.append(self.links.send(own, self.second.at[half, half], device))

    def total(self, half):
        if half == 0:
            for copy in self.near:
                copy.wait_recv()
        own = self.view(self.block(0), half)[...].astype(F32)
        return own + self.second[0, half].astype(F32) + self.second[1, half].astype(F32)


def halves_of(ref, axis_dim, half_dim):
    extent = ref.shape[half_dim] // 2

    def view(block, half):
        index = [slice(None)] * len(ref.shape)
        index[half_dim] = pl.ds(half * extent, extent)
        index[axis_dim] = block
        return ref.at[tuple(index)]

    return view


def grads_kernel(
    n1t, n2t, hidt, gatet, upt, pgrad, mixedt, mlow, cot, small,
    gate_out, up_out, down_out, in_out, out_out, small_out,
    n2x, n2y, cotz, gx, uy, hz,
    g1, g1a, g1b, g2, g2a, g2b, ga,
    u1, u1a, u1b, u2, u2a, u2b, ua,
    d1, d1a, d1b, dt, d2, d2a, d2b,
    ia, ia1, ia2, ib, ib1, ib2, ic, ic1, ic2,
    oa, oa1, oa2, ob, ob1, ob2, oc, oc1, oc2,
    sm1, sm2,
    send_sem, recv_sem,
):
    place = Place()
    links = Links(send_sem, recv_sem)
    barrier = pltpu.get_barrier_semaphore()
    peers = [place.peer(axis, shift) for axis in "zxy" for shift in (1, 2, 3)]
    peers.append(place.sibling())
    for device in peers:
        pl.semaphore_signal(barrier, inc=1, device_id=device, device_id_type=MESH)
    pl.semaphore_wait(barrier, len(peers))
    head = place.head

    gathered = {}
    traded = {}
    for axis, src, dst in (("z", cot, cotz), ("x", n2t, n2x), ("y", n2t, n2y)):
        for shift in (1, 3, 2):
            gathered[axis, shift] = links.send(
                src.at[pl.ds(2 * head, 2)], dst.at[shift - 1, pl.ds(2 * head, 2)], place.peer(axis, shift)
            )
    for axis, src, dst in (("z", hidt, hz), ("x", gatet, gx), ("y", upt, uy)):
        for shift in (1, 3, 2):
            block = lax.rem(place.coord[axis] + shift, 4)
            traded[axis, shift] = links.send(src.at[block], dst.at[shift - 1], place.peer(axis, shift))

    small_links = [links.send(small, sm1.at[0, shift - 1], place.peer("z", shift)) for shift in (1, 3, 2)]

    in_rings = [
        Ring(place, links, "z", lambda b, h: ia.at[0, b, pl.ds(2 * h, 2)], ia1.at[0], ia2.at[0]),
        Ring(place, links, "x", lambda b, h: ia.at[1, pl.ds(2 * h, 2), b], ia1.at[1], ia2.at[1]),
        Ring(place, links, "y", lambda b, h: ia.at[2, pl.ds(2 * h, 2), :, b], ia1.at[2], ia2.at[2]),
    ]
    for part in range(3):
        def in_tile(i, carry, part=part):
            res = jnp.dot(n1t[i], pgrad[:, part * 512:(part + 1) * 512], preferred_element_type=F32)
            ia[part, i] = res.astype(BF16).reshape(4, 4, 16, 512)
            return carry

        lax.fori_loop(0, 4, in_tile, 0)
        in_rings[part].start()

    def out_tile(i, carry):
        res = jnp.dot(mixedt[i], mlow[...], preferred_element_type=F32)
        oa[i] = res.astype(BF16).reshape(8, 16, 1024)
        return carry

    lax.fori_loop(0, 4, out_tile, 0)
    out_ring = Ring(place, links, "z", halves_of(oa, 0, 1), oa1, oa2)
    out_ring.start()

    shared = {}
    for axis, dst in (("z", cotz), ("x", n2x), ("y", n2y)):
        for shift in (1, 3, 2):
            gathered[axis, shift].wait_recv()
            here = dst.at[shift - 1, pl.ds(2 * head, 2)]
            shared[axis, shift] = links.send(here, here, place.sibling())

    for ring in in_rings:
        ring.pass_on()
    out_ring.pass_on()

    for copy in small_links:
        copy.wait_recv()
    sm2[0] = small[...] + sm1[0, 0] + sm1[0, 1] + sm1[0, 2]
    small_links = [links.send(sm2.at[0], sm1.at[1, shift - 1], place.peer("x", shift)) for shift in (1, 3, 2)]

    def ready(axis):
        for shift in (1, 3, 2):
            shared[axis, shift].wait_recv()
            traded[axis, shift].wait_recv()

    def wide(own_x, got_x, own_g, got_g, me, store):
        def tile(i, carry):
            res = lax.dot_general(own_x[i], own_g[me], NT, preferred_element_type=F32)
            for d in range(3):
                res += lax.dot_general(got_x[d, i], got_g[d], NT, preferred_element_type=F32)
            store(i, res.astype(BF16))
            return carry

        lax.fori_loop(0, 4, tile, 0)

    ready("z")

    def down_tile(i, carry):
        res = jnp.dot(
            hidt[place.coord["z"], i], cot[...].reshape(256, 1024), preferred_element_type=F32
        )
        for d in range(3):
            res += jnp.dot(hz[d, i], cotz[d].reshape(256, 1024), preferred_element_type=F32)
        d1[i] = res.astype(BF16).reshape(9, 16, 1024)
        return carry

    lax.fori_loop(0, 4, down_tile, 0)
    down_ring = Ring(place, links, "x", halves_of(d1, 0, 3), d1a, d1b)
    down_ring.start()

    ready("x")

    def gate_store(i, res):
        g1[pl.ds(4 * i, 4)] = res.reshape(4, 4, 16, 576)

    wide(n2t, n2x, gatet, gx, place.coord["x"], gate_store)
    gate_ring = Ring(place, links, "y", halves_of(g1, 1, 0), g1a, g1b)
    gate_ring.start()

    ready("y")

    def up_store(i, res):
        u1[i] = res.reshape(16, 16, 576)

    wide(n2t, n2y, upt, uy, place.coord["y"], up_store)
    up_ring = Ring(place, links, "z", halves_of(u1, 0, 1), u1a, u1b)
    up_ring.start()

    for half in range(2):
        ib[0, pl.ds(2 * half, 2)] = in_rings[0].total(half).astype(BF16)
    for half in range(2):
        ib[1, pl.ds(2 * half, 2)] = in_rings[1].total(half).astype(BF16)
    for half in range(2):
        ib[2, pl.ds(2 * half, 2)] = in_rings[2].total(half).astype(BF16)
    in_rings = [
        Ring(place, links, "x", halves_of(ib.at[0], 0, 1), ib1.at[0], ib2.at[0]),
        Ring(place, links, "y", halves_of(ib.at[1], 1, 0), ib1.at[1], ib2.at[1]),
        Ring(place, links, "z", halves_of(ib.at[2], 0, 1), ib1.at[2], ib2.at[2]),
    ]
    for ring in in_rings:
        ring.start()
    for half in range(2):
        ob[pl.ds(2 * half, 2)] = out_ring.total(half).astype(BF16).reshape(2, 2, 16, 1024)
    out_ring = Ring(place, links, "x", halves_of(ob, 0, 1), ob1, ob2)
    out_ring.start()

    down_ring.pass_on()
    gate_ring.pass_on()
    up_ring.pass_on()
    for ring in in_rings:
        ring.pass_on()
    out_ring.pass_on()

    for copy in small_links:
        copy.wait_recv()
    sm2[1] = sm2[0] + sm1[1, 0] + sm1[1, 1] + sm1[1, 2]
    small_links = [links.send(sm2.at[1], sm1.at[2, shift - 1], place.peer("y", shift)) for shift in (1, 3, 2)]

    dt[pl.ds(144, 16), :] = jnp.zeros((16, 1024), F32)
    for half in range(2):
        dt[pl.ds(0, 144), half * 512:(half + 1) * 512] = down_ring.total(half).reshape(144, 512)
    for y in range(4):
        d2[y] = dt[pl.ds(36 * y, 48), :].astype(BF16)
    down_ring = Ring(place, links, "y", halves_of(d2, 0, 2), d2a, d2b)
    down_ring.start()
    for half in range(2):
        g2[pl.ds(2 * half, 2)] = gate_ring.total(half).astype(BF16).reshape(2, 4, 16, 576)
    gate_ring = Ring(place, links, "z", halves_of(g2, 0, 1), g2a, g2b)
    gate_ring.start()
    for half in range(2):
        u2[pl.ds(2 * half, 2)] = up_ring.total(half).astype(BF16).reshape(2, 4, 16, 576)
    up_ring = Ring(place, links, "x", halves_of(u2, 0, 1), u2a, u2b)
    up_ring.start()
    for part in range(3):
        for half in range(2):
            ic[part, pl.ds(2 * half, 2)] = in_rings[part].total(half).astype(BF16)
    in_rings = [
        Ring(place, links, axis, halves_of(ic.at[part], 0, 2), ic1.at[part], ic2.at[part])
        for part, axis in enumerate("yzx")
    ]
    for ring in in_rings:
        ring.start()
    for half in range(2):
        res = out_ring.total(half).reshape(16, 1024).astype(BF16)
        for y in range(2):
            oc[2 * half + y] = jnp.concatenate([res[8 * y:8 * y + 8]] * 2, axis=0)
    out_ring = Ring(place, links, "y", halves_of(oc, 0, 2), oc1, oc2)
    out_ring.start()

    gate_ring.pass_on()
    up_ring.pass_on()
    down_ring.pass_on()
    for ring in in_rings:
        ring.pass_on()
    out_ring.pass_on()

    trades = []
    for ring, axis, own in ((gate_ring, "x", ga), (up_ring, "y", ua)):
        for half in range(2):
            own[0, pl.ds(2 * half, 2)] = ring.total(half)
        for shift in (1, 3, 2):
            block = lax.rem(place.coord[axis] + shift, 4)
            trades.append(
                links.send(own.at[0, block], own.at[1, place.coord[axis]], place.peer(axis, shift))
            )
    for half in range(2):
        down_out[:, half * 512:(half + 1) * 512] = down_ring.total(half)[:36]
    for part in range(3):
        for half in range(2):
            in_out[part, :, half * 256:(half + 1) * 256] = in_rings[part].total(half)
    for half in range(2):
        out_out[:, half * 512:(half + 1) * 512] = out_ring.total(half)[:8]
    for copy in small_links:
        copy.wait_recv()
    small_out[...] = sm2[1] + sm1[2, 0] + sm1[2, 1] + sm1[2, 2]
    for copy in trades:
        copy.wait_recv()
    for own, axis, out in ((ga, "x", gate_out), (ua, "y", up_out)):
        me = place.coord[axis]
        own[1, me] = own[0, me]
        out[...] = jnp.concatenate([own[1, p] for p in range(4)], axis=1)
    links.close()


def weight_grads(n1t, n2t, hidt, gatet, upt, pgrad, mixedt, mlow, cot, small):
    v = lambda *shape: pltpu.VMEM(shape, BF16)
    f = lambda *shape: pltpu.VMEM(shape, F32)

    def ring(*half):
        return [v(2, *half), v(2, 2, *half)]

    scratch = [
        v(3, 4, 256, 256), v(3, 4, 256, 256), v(3, 4, 64, 1024),
        v(3, 576, 256), v(3, 576, 256), v(3, 4, 144, 256),
        v(16, 4, 16, 576), *ring(8, 16, 576), v(4, 4, 16, 576), *ring(2, 16, 576), f(2, 4, 16, 576),
        v(4, 16, 16, 576), *ring(8, 16, 576), v(4, 4, 16, 576), *ring(2, 16, 576), f(2, 4, 16, 576),
        v(4, 9, 16, 1024), *ring(9, 16, 512), f(160, 1024), v(4, 48, 1024), *ring(48, 512),
        v(3, 4, 4, 4, 16, 512), v(3, 2, 2, 4, 16, 512), v(3, 2, 2, 2, 4, 16, 512),
        v(3, 4, 4, 16, 512), v(3, 2, 2, 16, 512), v(3, 2, 2, 2, 16, 512),
        v(3, 4, 16, 512), v(3, 2, 16, 256), v(3, 2, 2, 16, 256),
        v(4, 8, 16, 1024), *ring(4, 16, 1024),
        v(4, 2, 16, 1024), *ring(1, 16, 1024),
        v(4, 16, 1024), *ring(16, 512),
        f(3, 3, 8, 1024), f(2, 8, 1024),
        pltpu.SemaphoreType.DMA((N_SEMS,)), pltpu.SemaphoreType.DMA((N_SEMS,)),
    ]
    vmem = pl.BlockSpec(memory_space=pltpu.VMEM)
    return pl.pallas_call(
        grads_kernel,
        out_shape=[
            jax.ShapeDtypeStruct(shape, F32)
            for shape in ((16, 2304), (16, 2304), (36, 1024), (3, 16, 512), (8, 1024), (8, 1024))
        ],
        in_specs=[vmem] * 10,
        out_specs=[vmem] * 6,
        scratch_shapes=scratch,
        compiler_params=pltpu.CompilerParams(
            collective_id=0, has_side_effects=True, vmem_limit_bytes=56 * 2**20
        ),
        name="weight_grads",
    )(
        n1t.reshape(4, 256, 256), n2t.reshape(4, 256, 256), hidt.reshape(4, 4, 144, 256),
        gatet.reshape(4, 576, 256), upt.reshape(4, 576, 256), pgrad, mixedt.reshape(4, 128, 256),
        mlow, cot.reshape(4, 64, 1024), small,
    )


def passed_along(value, axis, steps):
    count = lax.axis_size(axis)
    initial, last = (max(0, -steps), min(count, count - steps))
    return lax.ppermute(value, axis, [(source, source + steps) for source in range(initial, last)])


def from_other(value):
    return lax.ppermute(value, "head", [(0, 1), (1, 0)])


def rms_scale(values):
    return lax.rsqrt(jnp.mean(values * values, axis=-1, keepdims=True) + EPS)


def norm_back(unit_grad, unit, scale):
    return scale * (unit_grad - unit * jnp.mean(unit_grad * unit, axis=-1, keepdims=True))


def shards(
    hidden_in,
    norm1_gain,
    in_weight,
    conv_weight,
    out_weight,
    norm2_gain,
    gate_weight,
    up_weight,
    down_weight,
    cotangent,
):
    tokens_here = hidden_in.shape[0]
    features = hidden_in.shape[1]
    channels = in_weight.shape[2]
    f32 = jnp.float32
    bf16 = jnp.bfloat16
    seq_length = min(SEQ_BASE, tokens_here * lax.axis_size("seq"))
    place = lax.axis_index("seq")
    first_pos = place * tokens_here
    carried = jnp.where(first_pos % seq_length != 0, 1.0, 0.0).astype(f32)
    inputs = hidden_in.astype(f32)
    scale_one = rms_scale(inputs)
    unit_one = inputs * scale_one
    normed_one = (unit_one * norm1_gain).astype(bf16)
    in_matrix = in_weight.reshape(features, 3 * channels)
    projected = jnp.dot(normed_one, in_matrix, preferred_element_type=f32)
    b_part = projected[:, :channels]
    c_part = projected[:, channels : 2 * channels]
    x_part = projected[:, 2 * channels :]
    gated = (b_part * x_part).astype(bf16)
    state = passed_along(gated[-2:], "seq", 1).astype(f32) * carried
    extended = jnp.concatenate([state, gated.astype(f32)], axis=0)
    convolved = (
        conv_weight[:, 0] * extended[:-2]
        + conv_weight[:, 1] * extended[1:-1]
        + conv_weight[:, 2] * extended[2:]
    )
    mixed = (c_part * convolved).astype(bf16)
    branch = jnp.dot(mixed, out_weight, preferred_element_type=f32)
    branch = branch + from_other(branch)
    middle = inputs + branch
    scale_two = rms_scale(middle)
    unit_two = middle * scale_two
    normed_two = (unit_two * norm2_gain).astype(bf16)
    gate_pre = jnp.dot(normed_two, gate_weight, preferred_element_type=f32)
    up_pre = jnp.dot(normed_two, up_weight, preferred_element_type=f32)
    sigmoid_gate = jax.nn.sigmoid(gate_pre)
    activated = gate_pre * sigmoid_gate
    hidden = (activated * up_pre).astype(bf16)
    ffn_part = jnp.dot(hidden, down_weight, preferred_element_type=f32).astype(bf16)
    ffn_out = ffn_part.astype(f32) + from_other(ffn_part).astype(f32)
    block_out = (middle + ffn_out).astype(bf16)
    cot_full = cotangent.astype(f32)
    hidden_grad = jnp.einsum("td,fd->tf", cotangent, down_weight, preferred_element_type=f32)
    gate_grad = (
        hidden_grad * up_pre * sigmoid_gate * (1.0 + gate_pre * (1.0 - sigmoid_gate))
    ).astype(bf16)
    up_grad = (hidden_grad * activated).astype(bf16)
    normed_two_part = jnp.einsum("tf,df->td", gate_grad, gate_weight, preferred_element_type=f32)
    normed_two_part = normed_two_part + jnp.einsum(
        "tf,df->td", up_grad, up_weight, preferred_element_type=f32
    )
    normed_two_part = normed_two_part.astype(bf16)
    normed_two_grad = normed_two_part.astype(f32) + from_other(normed_two_part).astype(f32)
    gain_two_grad = jnp.sum(normed_two_grad * unit_two, axis=0)
    middle_grad = cot_full + norm_back(normed_two_grad * norm2_gain, unit_two, scale_two)
    middle_low = middle_grad.astype(bf16)
    mixed_grad = jnp.einsum("td,kd->tk", middle_low, out_weight, preferred_element_type=f32)
    c_grad = mixed_grad * convolved
    convolved_grad = mixed_grad * c_part
    conv_w_grad = [
        jnp.sum(convolved_grad * extended[tap : tap + tokens_here], axis=0) for tap in range(3)
    ]
    zero_pair = jnp.zeros((2, channels), f32)
    grad_padded = jnp.concatenate([zero_pair, convolved_grad, zero_pair], axis=0)
    extended_grad = (
        conv_weight[:, 0] * grad_padded[2:]
        + conv_weight[:, 1] * grad_padded[1:-1]
        + conv_weight[:, 2] * grad_padded[:-2]
    )
    sent_back = passed_along(extended_grad[:2] * carried, "seq", -1)
    gated_grad = extended_grad[2:] + jnp.concatenate(
        [jnp.zeros((tokens_here - 2, channels), f32), sent_back], axis=0
    )
    projected_grad = jnp.concatenate(
        [gated_grad * x_part, c_grad, gated_grad * b_part], axis=1
    ).astype(bf16)
    normed_one_part = jnp.einsum(
        "tc,dc->td", projected_grad, in_matrix, preferred_element_type=f32
    ).astype(bf16)
    normed_one_grad = normed_one_part.astype(f32) + from_other(normed_one_part).astype(f32)
    gain_one_grad = jnp.sum(normed_one_grad * unit_one, axis=0)
    input_grad = (
        middle_grad + norm_back(normed_one_grad * norm1_gain, unit_one, scale_one)
    ).astype(bf16)
    pad = jnp.zeros((features - channels,), f32)
    empty = jnp.zeros((features,), f32)
    small = jnp.stack(
        [gain_one_grad, gain_two_grad]
        + [jnp.concatenate([tap, pad]) for tap in conv_w_grad]
        + [empty] * 3
    )
    gate_final, up_final, down_final, in_final, out_final, small_final = weight_grads(
        normed_one.T, normed_two.T, hidden.T, gate_grad.T, up_grad.T,
        projected_grad, mixed.T, middle_low, cotangent, small,
    )
    gains = lax.dynamic_slice(small_final, (0, place * 16), (2, 16))
    conv_final = lax.dynamic_slice(small_final, (2, place * 8), (3, 8)).T
    return (
        block_out,
        input_grad,
        gains[0],
        in_final.transpose(1, 0, 2),
        conv_final,
        out_final,
        gains[1],
        gate_final,
        up_final,
        down_final,
    )


def solution(mesh):
    placed = (
        P("seq", None),
        P(),
        P(None, None, "head"),
        P("head", None),
        P("head", None),
        P(),
        P(None, "head"),
        P(None, "head"),
        P("head", None),
        P("seq", None),
    )
    return jax.shard_map(
        shards,
        mesh=mesh,
        in_specs=placed,
        out_specs=(
            P("seq", None),
            P("seq", None),
            P("seq"),
            P("seq", None, "head"),
            P(("head", "seq"), None),
            P(("head", "seq"), None),
            P("seq"),
            P("seq", "head"),
            P("seq", "head"),
            P(("head", "seq"), None),
        ),
        check_vma=False,
    )
```

```python
import jax
import jax.numpy as jnp
from jax import lax
from jax.experimental import pallas as pl
from jax.experimental.pallas import tpu as pltpu
from jax.sharding import PartitionSpec as P

EPS = 1e-05
MESH = pl.DeviceIdType.MESH
F32 = jnp.float32
BF16 = jnp.bfloat16
NT = (((1,), (1,)), ((), ()))
N_SEMS = 180
TILE = 768


class Place:
    def __init__(self):
        self.seq = lax.axis_index("seq")
        self.head = lax.axis_index("head")
        self.coord = {
            "z": lax.div(self.seq, 16),
            "x": lax.rem(lax.div(self.seq, 4), 4),
            "y": lax.rem(self.seq, 4),
        }

        self.blocks = {
            axis: [self.coord[axis]] + [lax.rem(self.coord[axis] + shift, 4) for shift in (1, 2, 3)]
            for axis in "zxy"
        }
        self.peers = {}
        for axis in "zxy":
            for shift in (1, 2, 3):
                moved = dict(self.coord)
                moved[axis] = self.blocks[axis][shift]
                self.peers[axis, shift] = ((moved["z"] * 4 + moved["x"]) * 4 + moved["y"], self.head)
        self.along = {
            shift: (lax.rem(self.seq + 64 + shift, 64), self.head) for shift in (1, -1)
        }

    def peer(self, axis, shift):
        return self.peers[axis, shift]

    def sibling(self):
        return (self.seq, 1 - self.head)


class Links:
    def __init__(self, send_sem, recv_sem):
        self.send_sem = send_sem
        self.recv_sem = recv_sem
        self.used = 0
        self.open = []

    def plan(self, src, dst, device):
        copy = pltpu.make_async_remote_copy(
            src_ref=src,
            dst_ref=dst,
            send_sem=self.send_sem.at[self.used],
            recv_sem=self.recv_sem.at[self.used],
            device_id=device,
            device_id_type=MESH,
        )
        self.used += 1
        return copy

    def send(self, src, dst, device):
        copy = self.plan(src, dst, device)
        copy.start()
        self.open.append(copy)
        return copy

    def close(self):
        for copy in self.open:
            copy.wait_send()
        self.open = []


class Ring:
    def __init__(self, place, links, axis, view, first, second):
        self.place, self.links, self.axis, self.view = place, links, axis, view
        self.first, self.second = first, second
        self.me = place.coord[axis]

    def block(self, shift):
        return self.place.blocks[self.axis][shift]

    def start(self):
        right, left = self.place.peer(self.axis, 1), self.place.peer(self.axis, 3)
        send = self.links.send
        self.far = [
            send(self.view(self.block(2), 0), self.first.at[0], right),
            send(self.view(self.block(2), 1), self.first.at[1], left),
        ]
        self.near = [
            send(self.view(self.block(1), 1), self.second.at[0, 1], right),
            send(self.view(self.block(3), 0), self.second.at[1, 0], left),
        ]

    def pass_on(self):
        right, left = self.place.peer(self.axis, 1), self.place.peer(self.axis, 3)
        for half, shift, device in ((0, 1, right), (1, 3, left)):
            self.far[half].wait_recv()
            own = self.view(self.block(shift), half)
            own[...] = (own[...].astype(F32) + self.first[half].astype(F32)).astype(BF16)
            self.near.append(self.links.send(own, self.second.at[half, half], device))

    def total(self, half):
        if half == 0:
            for copy in self.near:
                copy.wait_recv()
        own = self.view(self.block(0), half)[...].astype(F32)
        return own + self.second[0, half].astype(F32) + self.second[1, half].astype(F32)


def halves_of(ref, axis_dim, half_dim):
    extent = ref.shape[half_dim] // 2

    def view(block, half):
        index = [slice(None)] * len(ref.shape)
        index[half_dim] = pl.ds(half * extent, extent)
        index[axis_dim] = block
        return ref.at[tuple(index)]

    return view


def in_rows(extent, step, body, carry=0):
    def one(i, carry):
        return body(pl.multiple_of(i * step, step), carry)

    return lax.fori_loop(0, extent // step, one, carry)


def mean_square(values):
    return jnp.mean(values * values, axis=-1, keepdims=True)


def block_kernel(
    hin, gain1, w_in, w_conv, w_out, gain2, w_gate, w_up, w_down, cot,
    block_out, input_grad, gate_out, up_out, down_out, in_out, out_out, small_out,
    win, wout, n1, n1t, n2, n2t, hidt, gatet, upt, proj, gbuf, cv, mixed, mixedt, mid, mlow, cgbuf, mxg, pg,
    small, xb, xf, xn, xh,
    n2x, n2y, cotz, gx, uy, hz,
    g1a, g1b, g2a, g2b, ga,
    u1a, u1b, u2a, u2b, ua,
    d1a, d1b, d2a, d2b,
    ia1, ia2, ib1, ib2, ic1, ic2,
    oa1, oa2, ob1, ob2, oc1, oc2,
    sm1, sm2,
    send_sem, recv_sem, load_sem,
):
    place = Place()
    links = Links(send_sem, recv_sem)
    head = place.head
    barrier = pltpu.get_barrier_semaphore()
    peers = [place.peer(axis, shift) for axis in "zxy" for shift in (1, 2, 3)]
    peers += [place.sibling(), place.along[1], place.along[-1]]
    carried = jnp.where(lax.rem(place.seq, 16) != 0, 1.0, 0.0).astype(F32)
    carried_on = jnp.where(lax.rem(place.seq, 16) != 15, 1.0, 0.0).astype(F32)
    gathered = {}
    traded = {}
    shared = {}

    for axis, src, dst in (("z", cot, cotz), ("x", n2t, n2x), ("y", n2t, n2y)):
        part = src.shape[0] // 2
        mine = pl.ds(part * head, part)
        for shift in (1, 3, 2):
            gathered[axis, shift] = links.plan(
                src.at[mine], dst.at[shift - 1, mine], place.peer(axis, shift)
            )

    def gather(axis):
        for shift in (1, 3, 2):
            gathered[axis, shift].start()

    def trade(axis, src, dst):
        for shift in (1, 3, 2):
            block = place.blocks[axis][shift]
            rows = pl.ds(pl.multiple_of(block * 576, 576), 576)
            traded[axis, shift] = links.send(src.at[rows], dst.at[shift - 1], place.peer(axis, shift))

    def share(axis, dst):
        for shift in (1, 3, 2):
            gathered[axis, shift].wait_recv()
            part = dst.shape[1] // 2
            here = dst.at[shift - 1, pl.ds(part * head, part)]
            shared[axis, shift] = links.send(here, here, place.sibling())

    taps = w_conv[...]

    def shifted_gated(r):
        window = gbuf[pl.ds(r, 48), :].astype(F32)
        return [pltpu.roll(window, 2, 0)[16:], pltpu.roll(window, 1, 0)[16:], window[16:]]

    def forward(wg, wu, wd, pre_g, pre_u, grad_h, hid_s, gg_s, ug_s, ffn_acc, n2g_acc):
        loads = []
        for src, dst in (
            (w_in.at[0], win.at[0]), (w_in.at[1], win.at[1]), (w_in.at[2], win.at[2]),
            (w_out, wout), (w_gate, wg), (w_up, wu), (w_down, wd),
        ):
            copy = pltpu.make_async_copy(src, dst, load_sem.at[len(loads)])
            copy.start()
            loads.append(copy)
        for device in peers:
            pl.semaphore_signal(barrier, inc=1, device_id=device, device_id_type=MESH)

        def norm_one(r, carry):
            x = hin[pl.ds(r, 32), :].astype(F32)
            n1[pl.ds(r, 32), :] = (x * lax.rsqrt(mean_square(x) + EPS) * gain1[...]).astype(BF16)
            return carry

        in_rows(256, 32, norm_one)
        pl.semaphore_wait(barrier, len(peers))
        gather("z")
        for part in (0, 2, 1):
            loads[part].wait()
            proj[part] = jnp.dot(n1[...], win[part], preferred_element_type=F32)
            if part == 2:
                def gate_rows(r, carry):
                    here = pl.ds(r, 32)
                    gbuf[pl.ds(r + 16, 32), :] = (proj[0, here, :] * proj[2, here, :]).astype(BF16)
                    return carry

                in_rows(256, 32, gate_rows)
                edge = links.send(gbuf.at[pl.ds(256, 16)], gbuf.at[pl.ds(0, 16)], place.along[1])
        for i in range(4):
            n1t[i] = n1[:, 256 * i:256 * i + 256].T
        loads[3].wait()
        edge.wait_recv()
        gbuf[pl.ds(0, 16), :] = (gbuf[pl.ds(0, 16), :].astype(F32) * carried).astype(BF16)

        def mix_rows(r, carry):
            here = pl.ds(r, 32)
            old, last, now = shifted_gated(r)
            value = taps[0:1] * old + taps[1:2] * last + taps[2:3] * now
            cv[here, :] = value
            mixed[here, :] = (proj[1, here, :] * value).astype(BF16)
            return carry

        in_rows(256, 32, mix_rows)
        branch = []
        for half in range(2):
            here = pl.ds(128 * half, 128)
            xb[0, here, :] = jnp.dot(mixed[here, :], wout[...], preferred_element_type=F32).astype(BF16)
            branch.append(links.send(xb.at[0, here], xb.at[1, here], place.sibling()))
        for i in range(4):
            mixedt[i] = mixed[:, 128 * i:128 * i + 128].T

        def norm_two(r, carry):
            here = pl.ds(r, 32)
            middle = hin[here, :].astype(F32) + (xb[0, here, :].astype(F32) + xb[1, here, :].astype(F32))
            mid[here, :] = middle
            n2[here, :] = (middle * lax.rsqrt(mean_square(middle) + EPS) * gain2[...]).astype(BF16)
            return carry

        for half in range(2):
            branch[half].wait_recv()
            in_rows(128, 32, lambda r, carry: norm_two(r + 128 * half, carry))
        for i in range(4):
            n2t[i] = n2[:, 256 * i:256 * i + 256].T
        gather("x")
        gather("y")
        for copy in loads[4:]:
            copy.wait()
        cot_here = cot[...].reshape(256, 1024)
        for t in range(0, 2304, TILE):
            cut = slice(t, t + TILE)
            pre_g[...] = jnp.dot(n2[...], wg[:, cut], preferred_element_type=F32)
            pre_u[...] = jnp.dot(n2[...], wu[:, cut], preferred_element_type=F32)
            grad_h[...] = lax.dot_general(cot_here, wd[cut, :], NT, preferred_element_type=F32)

            def act_rows(r, carry):
                here = pl.ds(r, 32)
                gate, up, grad = pre_g[here, :], pre_u[here, :], grad_h[here, :]
                sig = jax.nn.sigmoid(gate)
                act = gate * sig
                hid_s[here, :] = (act * up).astype(BF16)
                gg_s[here, :] = (grad * up * (sig * (1.0 + gate * (1.0 - sig)))).astype(BF16)
                ug_s[here, :] = (grad * act).astype(BF16)
                return carry

            in_rows(256, 32, act_rows)
            hidt[cut, :] = hid_s[...].T
            gatet[cut, :] = gg_s[...].T
            upt[cut, :] = ug_s[...].T
            ffn = jnp.dot(hid_s[...], wd[cut, :], preferred_element_type=F32)
            back = lax.dot_general(gg_s[...], wg[:, cut], NT, preferred_element_type=F32)
            back += lax.dot_general(ug_s[...], wu[:, cut], NT, preferred_element_type=F32)
            last = t + TILE == 2304
            if t > 0:
                ffn += ffn_acc[...]
                back += n2g_acc[...]
            if last:
                xn[0] = back.astype(BF16)
                xf[0] = ffn.astype(BF16)
            else:
                ffn_acc[...] = ffn
                n2g_acc[...] = back
        links.close()

    v = lambda *shape: pltpu.VMEM(shape, BF16)
    f = lambda *shape: pltpu.VMEM(shape, F32)
    pl.run_scoped(
        forward, v(1024, 2304), v(1024, 2304), v(2304, 1024),
        f(256, TILE), f(256, TILE), f(256, TILE), v(256, TILE), v(256, TILE), v(256, TILE),
        f(256, 1024), f(256, 1024),
    )

    def backward(g1, g2, u1, u2, d1, dt, d2, ia, ib, ic, oa, ob, oc):
        back_link = links.send(xn.at[0], xn.at[1], place.sibling())
        trade("z", hidt, hz)
        trade("x", gatet, gx)
        trade("y", upt, uy)
        ffn_link = links.send(xf.at[0], xf.at[1], place.sibling())
        share("z", cotz)
        back_link.wait_recv()
        ffn_link.wait_recv()
        small[...] = jnp.zeros((8, 1024), F32)

        def norm_two_back(i, total):
            here = pl.ds(pl.multiple_of(i * 32, 32), 32)
            grad = xn[0, here, :].astype(F32) + xn[1, here, :].astype(F32)
            middle = mid[here, :]
            ffn = xf[0, here, :].astype(F32) + xf[1, here, :].astype(F32)
            block_out[here, :] = (middle + ffn).astype(BF16)
            scale = lax.rsqrt(mean_square(middle) + EPS)
            unit = middle * scale
            total += jnp.sum((grad * unit).reshape(4, 8, 1024), axis=0)
            inner = grad * gain2[...]
            inner = scale * (inner - unit * jnp.mean(inner * unit, axis=-1, keepdims=True))
            middle = cot[i].astype(F32) + inner
            mid[here, :] = middle
            mlow[here, :] = middle.astype(BF16)
            return total

        total = lax.fori_loop(0, 8, norm_two_back, jnp.zeros((8, 1024), F32))
        small[1:2, :] = jnp.sum(total, axis=0, keepdims=True)
        mxg[...] = lax.dot_general(mlow[...], wout[...], NT, preferred_element_type=F32)

        def conv_back(r, totals):
            here = pl.ds(r, 32)
            grad = mxg[here, :]
            back = grad * proj[1, here, :]
            cgbuf[here, :] = back
            pg[here, 512:1024] = (grad * cv[here, :]).astype(BF16)
            return tuple(
                t + jnp.sum((back * g).reshape(4, 8, 512), axis=0) for t, g in zip(totals, shifted_gated(r))
            )

        totals = in_rows(256, 32, conv_back, (jnp.zeros((8, 512), F32),) * 3)
        edge = links.send(cgbuf.at[pl.ds(0, 8)], cgbuf.at[pl.ds(256, 8)], place.along[-1])
        for k in range(3):
            small[2 + k:3 + k, 0:512] = jnp.sum(totals[k], axis=0, keepdims=True)

        def out_tile(i, carry):
            res = jnp.dot(mixedt[i], mlow[...], preferred_element_type=F32)
            oa[i] = res.astype(BF16).reshape(8, 16, 1024)
            return carry

        lax.fori_loop(0, 4, out_tile, 0)
        out_ring = Ring(place, links, "z", halves_of(oa, 0, 1), oa1, oa2)
        out_ring.start()
        edge.wait_recv()
        cgbuf[pl.ds(256, 8), :] = cgbuf[pl.ds(256, 8), :] * carried_on

        def taps_back(r, carry):
            here = pl.ds(r, 32)
            window = cgbuf[pl.ds(r, 40), :]
            grad = (
                taps[2:3] * window[:32]
                + taps[1:2] * pltpu.roll(window, 39, 0)[:32]
                + taps[0:1] * pltpu.roll(window, 38, 0)[:32]
            )
            pg[here, 0:512] = (grad * proj[2, here, :]).astype(BF16)
            pg[here, 1024:1536] = (grad * proj[0, here, :]).astype(BF16)
            return carry

        in_rows(256, 32, taps_back)
        part = lax.dot_general(pg[:, 0:512], win[0], NT, preferred_element_type=F32)
        part += lax.dot_general(pg[:, 512:1024], win[1], NT, preferred_element_type=F32)
        part += lax.dot_general(pg[:, 1024:1536], win[2], NT, preferred_element_type=F32)
        xh[0] = part.astype(BF16)
        first_link = links.send(xh.at[0], xh.at[1], place.sibling())

        in_rings = [
            Ring(place, links, "z", lambda b, h: ia.at[0, b, pl.ds(2 * h, 2)], ia1.at[0], ia2.at[0]),
            Ring(place, links, "x", lambda b, h: ia.at[1, pl.ds(2 * h, 2), b], ia1.at[1], ia2.at[1]),
            Ring(place, links, "y", lambda b, h: ia.at[2, pl.ds(2 * h, 2), :, b], ia1.at[2], ia2.at[2]),
        ]
        for part in range(3):
            def in_tile(i, carry, part=part):
                res = jnp.dot(n1t[i], pg[:, part * 512:(part + 1) * 512], preferred_element_type=F32)
                ia[part, i] = res.astype(BF16).reshape(4, 4, 16, 512)
                return carry

            lax.fori_loop(0, 4, in_tile, 0)
            in_rings[part].start()

        def ready(axis):
            for shift in (1, 3, 2):
                shared[axis, shift].wait_recv()
                traded[axis, shift].wait_recv()

        share("x", n2x)
        share("y", n2y)
        first_link.wait_recv()

        def norm_one_back(r, total):
            here = pl.ds(r, 32)
            grad = xh[0, here, :].astype(F32) + xh[1, here, :].astype(F32)
            x = hin[here, :].astype(F32)
            scale = lax.rsqrt(mean_square(x) + EPS)
            unit = x * scale
            total += jnp.sum((grad * unit).reshape(4, 8, 1024), axis=0)
            inner = grad * gain1[...]
            inner = scale * (inner - unit * jnp.mean(inner * unit, axis=-1, keepdims=True))
            input_grad[here, :] = (mid[here, :] + inner).astype(BF16)
            return total

        total = in_rows(256, 32, norm_one_back, jnp.zeros((8, 1024), F32))
        small[0:1, :] = jnp.sum(total, axis=0, keepdims=True)
        small_links = [links.send(small, sm1.at[0, shift - 1], place.peer("z", shift)) for shift in (1, 3, 2)]

        def wide(own_x, got_x, own_g, got_g, me, store):
            def tile(i, carry):
                own = own_g[pl.ds(pl.multiple_of(me * 576, 576), 576), :]
                res = lax.dot_general(own_x[i], own, NT, preferred_element_type=F32)
                for d in range(3):
                    res += lax.dot_general(got_x[d, i], got_g[d], NT, preferred_element_type=F32)
                store(i, res.astype(BF16))
                return carry

            lax.fori_loop(0, 4, tile, 0)

        ready("z")

        def down_tile(i, carry):
            own = hidt[pl.ds(pl.multiple_of(place.coord["z"] * 576 + i * 144, 144), 144), :]
            res = jnp.dot(own, cot[...].reshape(256, 1024), preferred_element_type=F32)
            for d in range(3):
                got = hz[d, pl.ds(pl.multiple_of(i * 144, 144), 144), :]
                res += jnp.dot(got, cotz[d].reshape(256, 1024), preferred_element_type=F32)
            d1[i] = res.astype(BF16).reshape(9, 16, 1024)
            return carry

        lax.fori_loop(0, 4, down_tile, 0)
        down_ring = Ring(place, links, "x", halves_of(d1, 0, 3), d1a, d1b)
        down_ring.start()

        ready("x")

        def gate_store(i, res):
            g1[pl.ds(4 * i, 4)] = res.reshape(4, 4, 16, 576)

        wide(n2t, n2x, gatet, gx, place.coord["x"], gate_store)
        gate_ring = Ring(place, links, "y", halves_of(g1, 1, 0), g1a, g1b)
        gate_ring.start()

        ready("y")

        def up_store(i, res):
            u1[i] = res.reshape(16, 16, 576)

        wide(n2t, n2y, upt, uy, place.coord["y"], up_store)
        up_ring = Ring(place, links, "z", halves_of(u1, 0, 1), u1a, u1b)
        up_ring.start()

        for ring in in_rings:
            ring.pass_on()
        out_ring.pass_on()

        for copy in small_links:
            copy.wait_recv()
        sm2[0] = small[...] + sm1[0, 0] + sm1[0, 1] + sm1[0, 2]
        small_links = [links.send(sm2.at[0], sm1.at[1, shift - 1], place.peer("x", shift)) for shift in (1, 3, 2)]

        for half in range(2):
            ib[0, pl.ds(2 * half, 2)] = in_rings[0].total(half).astype(BF16)
        for half in range(2):
            ib[1, pl.ds(2 * half, 2)] = in_rings[1].total(half).astype(BF16)
        for half in range(2):
            ib[2, pl.ds(2 * half, 2)] = in_rings[2].total(half).astype(BF16)
        in_rings = [
            Ring(place, links, "x", halves_of(ib.at[0], 0, 1), ib1.at[0], ib2.at[0]),
            Ring(place, links, "y", halves_of(ib.at[1], 1, 0), ib1.at[1], ib2.at[1]),
            Ring(place, links, "z", halves_of(ib.at[2], 0, 1), ib1.at[2], ib2.at[2]),
        ]
        for ring in in_rings:
            ring.start()
        for half in range(2):
            ob[pl.ds(2 * half, 2)] = out_ring.total(half).astype(BF16).reshape(2, 2, 16, 1024)
        out_ring = Ring(place, links, "x", halves_of(ob, 0, 1), ob1, ob2)
        out_ring.start()

        down_ring.pass_on()
        gate_ring.pass_on()
        up_ring.pass_on()
        for ring in in_rings:
            ring.pass_on()
        out_ring.pass_on()

        for copy in small_links:
            copy.wait_recv()
        sm2[1] = sm2[0] + sm1[1, 0] + sm1[1, 1] + sm1[1, 2]
        small_links = [links.send(sm2.at[1], sm1.at[2, shift - 1], place.peer("y", shift)) for shift in (1, 3, 2)]

        dt[pl.ds(144, 16), :] = jnp.zeros((16, 1024), F32)
        for half in range(2):
            dt[pl.ds(0, 144), half * 512:(half + 1) * 512] = down_ring.total(half).reshape(144, 512)
        for y in range(4):
            d2[y] = dt[pl.ds(36 * y, 48), :].astype(BF16)
        down_ring = Ring(place, links, "y", halves_of(d2, 0, 2), d2a, d2b)
        down_ring.start()
        for half in range(2):
            g2[pl.ds(2 * half, 2)] = gate_ring.total(half).astype(BF16).reshape(2, 4, 16, 576)
        gate_ring = Ring(place, links, "z", halves_of(g2, 0, 1), g2a, g2b)
        gate_ring.start()
        for half in range(2):
            u2[pl.ds(2 * half, 2)] = up_ring.total(half).astype(BF16).reshape(2, 4, 16, 576)
        up_ring = Ring(place, links, "x", halves_of(u2, 0, 1), u2a, u2b)
        up_ring.start()
        for part in range(3):
            for half in range(2):
                ic[part, pl.ds(2 * half, 2)] = in_rings[part].total(half).astype(BF16)
        in_rings = [
            Ring(place, links, axis, halves_of(ic.at[part], 0, 2), ic1.at[part], ic2.at[part])
            for part, axis in enumerate("yzx")
        ]
        for ring in in_rings:
            ring.start()
        for half in range(2):
            res = out_ring.total(half).reshape(16, 1024).astype(BF16)
            for y in range(2):
                oc[2 * half + y] = jnp.concatenate([res[8 * y:8 * y + 8]] * 2, axis=0)
        out_ring = Ring(place, links, "y", halves_of(oc, 0, 2), oc1, oc2)
        out_ring.start()

        gate_ring.pass_on()
        up_ring.pass_on()
        down_ring.pass_on()
        for ring in in_rings:
            ring.pass_on()
        out_ring.pass_on()

        trades = []
        for ring, axis, own in ((gate_ring, "x", ga), (up_ring, "y", ua)):
            for half in range(2):
                own[0, pl.ds(2 * half, 2)] = ring.total(half)
            for shift in (1, 3, 2):
                block = place.blocks[axis][shift]
                trades.append(
                    links.send(own.at[0, block], own.at[1, place.coord[axis]], place.peer(axis, shift))
                )
        for half in range(2):
            down_out[:, half * 512:(half + 1) * 512] = down_ring.total(half)[:36]
        for part in range(3):
            for half in range(2):
                in_out[:, part, half * 256:(half + 1) * 256] = in_rings[part].total(half)
        for half in range(2):
            out_out[:, half * 512:(half + 1) * 512] = out_ring.total(half)[:8]
        for copy in small_links:
            copy.wait_recv()
        small_out[...] = sm2[1] + sm1[2, 0] + sm1[2, 1] + sm1[2, 2]
        for copy in trades:
            copy.wait_recv()
        for own, axis, out in ((ga, "x", gate_out), (ua, "y", up_out)):
            me = place.coord[axis]
            own[1, me] = own[0, me]
            out[...] = jnp.concatenate([own[1, p] for p in range(4)], axis=1)
        links.close()
        for copy in gathered.values():
            copy.wait_send()

    pl.run_scoped(
        backward,
        v(16, 4, 16, 576), v(4, 4, 16, 576), v(4, 16, 16, 576), v(4, 4, 16, 576),
        v(4, 9, 16, 1024), f(160, 1024), v(4, 48, 1024),
        v(3, 4, 4, 4, 16, 512), v(3, 4, 4, 16, 512), v(3, 4, 16, 512),
        v(4, 8, 16, 1024), v(4, 2, 16, 1024), v(4, 16, 1024),
    )


def finish_kernel(
    block_in, grad_in, gate_in, up_in, down_in, in_in, out_in, small_in,
    block_out, input_grad, gate_out, up_out, down_out, in_out, out_out, gain1_out, gain2_out, conv_out,
):
    place = lax.axis_index("seq")
    for src, dst in (
        (block_in, block_out), (grad_in, input_grad), (gate_in, gate_out), (up_in, up_out),
        (down_in, down_out), (in_in, in_out), (out_in, out_out),
    ):
        dst[...] = src[...]
    gains = pltpu.roll(small_in[...], 1024 - 16 * place, 1)
    gain1_out[...] = gains[0:1, 0:16]
    gain2_out[...] = gains[1:2, 0:16]
    taps = pltpu.roll(small_in[...], 1024 - 8 * place, 1)
    conv_out[...] = taps[:, 0:128].T[0:8, 2:5]


def shards(
    hidden_in, norm1_gain, in_weight, conv_weight, out_weight, norm2_gain, gate_weight, up_weight, down_weight,
    cotangent,
):
    v = lambda *shape: pltpu.VMEM(shape, BF16)
    f = lambda *shape: pltpu.VMEM(shape, F32)

    def ring(*half):
        return [v(2, *half), v(2, 2, *half)]

    scratch = [
        v(3, 1024, 512), v(512, 1024), v(256, 1024), v(4, 256, 256), v(256, 1024), v(4, 256, 256),
        v(2304, 256), v(2304, 256), v(2304, 256), f(3, 256, 512), v(272, 512), f(256, 512), v(256, 512),
        v(4, 128, 256), f(256, 1024), v(256, 1024), f(264, 512), f(256, 512), v(256, 1536), f(8, 1024),
        *[v(2, 256, 1024)] * 4,
        v(3, 4, 256, 256), v(3, 4, 256, 256), v(3, 8, 32, 1024),
        v(3, 576, 256), v(3, 576, 256), v(3, 576, 256),
        *ring(8, 16, 576), *ring(2, 16, 576), f(2, 4, 16, 576),
        *ring(8, 16, 576), *ring(2, 16, 576), f(2, 4, 16, 576),
        *ring(9, 16, 512), *ring(48, 512),
        v(3, 2, 2, 4, 16, 512), v(3, 2, 2, 2, 4, 16, 512),
        v(3, 2, 2, 16, 512), v(3, 2, 2, 2, 16, 512),
        v(3, 2, 16, 256), v(3, 2, 2, 16, 256),
        *ring(4, 16, 1024), *ring(1, 16, 1024), *ring(16, 512),
        f(3, 3, 8, 1024), f(2, 8, 1024),
        pltpu.SemaphoreType.DMA((N_SEMS,)), pltpu.SemaphoreType.DMA((N_SEMS,)), pltpu.SemaphoreType.DMA((7,)),
    ]
    vmem = pl.BlockSpec(memory_space=pltpu.VMEM)
    far = pl.BlockSpec(memory_space=pl.ANY)
    (
        block_out, input_grad, gate_final, up_final, down_final, in_final, out_final, small_final,
    ) = pl.pallas_call(
        block_kernel,
        out_shape=[jax.ShapeDtypeStruct((256, 1024), BF16)] * 2
        + [
            jax.ShapeDtypeStruct(shape, F32)
            for shape in ((16, 2304), (16, 2304), (36, 1024), (16, 3, 512), (8, 1024), (8, 1024))
        ],
        in_specs=[vmem, vmem, far, vmem, far, vmem, far, far, far, vmem],
        out_specs=[vmem] * 8,
        scratch_shapes=scratch,
        compiler_params=pltpu.CompilerParams(
            collective_id=0, has_side_effects=True, vmem_limit_bytes=62 * 2**20
        ),
        name="block",
    )(
        hidden_in, norm1_gain.reshape(1, 1024), in_weight.transpose(1, 0, 2), conv_weight.T, out_weight,
        norm2_gain.reshape(1, 1024), gate_weight, up_weight, down_weight, cotangent.reshape(8, 32, 1024),
    )
    (
        block_out, input_grad, gate_final, up_final, down_final, in_final, out_final, gain1_final, gain2_final,
        conv_final,
    ) = pl.pallas_call(
        finish_kernel,
        out_shape=[jax.ShapeDtypeStruct((256, 1024), BF16)] * 2
        + [
            jax.ShapeDtypeStruct(shape, F32)
            for shape in (
                (16, 2304), (16, 2304), (36, 1024), (16, 3, 512), (8, 1024), (1, 16), (1, 16), (8, 3),
            )
        ],
        in_specs=[vmem] * 8,
        out_specs=[vmem] * 10,
        name="finish",
    )(block_out, input_grad, gate_final, up_final, down_final, in_final, out_final, small_final)
    return (
        block_out,
        input_grad,
        gain1_final.reshape(16),
        in_final,
        conv_final,
        out_final,
        gain2_final.reshape(16),
        gate_final,
        up_final,
        down_final,
    )


def solution(mesh):
    placed = (
        P("seq", None),
        P(),
        P(None, None, "head"),
        P("head", None),
        P("head", None),
        P(),
        P(None, "head"),
        P(None, "head"),
        P("head", None),
        P("seq", None),
    )
    return jax.shard_map(
        shards,
        mesh=mesh,
        in_specs=placed,
        out_specs=(
            P("seq", None),
            P("seq", None),
            P("seq"),
            P("seq", None, "head"),
            P(("head", "seq"), None),
            P(("head", "seq"), None),
            P("seq"),
            P("seq", "head"),
            P("seq", "head"),
            P(("head", "seq"), None),
        ),
        check_vma=False,
    )
```

```python
import jax
import jax.numpy as jnp
from jax import lax
from jax.experimental import pallas as pl
from jax.experimental.pallas import tpu as pltpu
from jax.sharding import PartitionSpec as P

EPS = 1e-05
MESH = pl.DeviceIdType.MESH
F32 = jnp.float32
BF16 = jnp.bfloat16
NT = (((1,), (1,)), ((), ()))
N_SEMS = 210
TILE = 768
CUTS = (0, 256, 896, 1536)


class Place:
    def __init__(self):
        self.seq = lax.axis_index("seq")
        self.head = lax.axis_index("head")
        self.coord = {
            "z": lax.div(self.seq, 16),
            "x": lax.rem(lax.div(self.seq, 4), 4),
            "y": lax.rem(self.seq, 4),
        }

        self.blocks = {
            axis: [self.coord[axis]] + [lax.rem(self.coord[axis] + shift, 4) for shift in (1, 2, 3)]
            for axis in "zxy"
        }
        self.peers = {}
        for axis in "zxy":
            for shift in (1, 2, 3):
                moved = dict(self.coord)
                moved[axis] = self.blocks[axis][shift]
                self.peers[axis, shift] = ((moved["z"] * 4 + moved["x"]) * 4 + moved["y"], self.head)
        self.along = {
            shift: (lax.rem(self.seq + 64 + shift, 64), self.head) for shift in (1, -1)
        }

    def peer(self, axis, shift):
        return self.peers[axis, shift]

    def diagonal(self, first, shift, second, other):
        moved = dict(self.coord)
        moved[first] = self.blocks[first][shift]
        moved[second] = self.blocks[second][other]
        return ((moved["z"] * 4 + moved["x"]) * 4 + moved["y"], self.head)

    def sibling(self):
        return (self.seq, 1 - self.head)


class Links:
    def __init__(self, send_sem, recv_sem):
        self.send_sem = send_sem
        self.recv_sem = recv_sem
        self.used = 0
        self.open = []

    def plan(self, src, dst, device):
        copy = pltpu.make_async_remote_copy(
            src_ref=src,
            dst_ref=dst,
            send_sem=self.send_sem.at[self.used],
            recv_sem=self.recv_sem.at[self.used],
            device_id=device,
            device_id_type=MESH,
        )
        self.used += 1
        return copy

    def send(self, src, dst, device):
        copy = self.plan(src, dst, device)
        copy.start()
        self.open.append(copy)
        return copy

    def close(self):
        for copy in self.open:
            copy.wait_send()
        self.open = []


class Ring:
    def __init__(self, place, links, axis, view, first, second):
        self.place, self.links, self.axis, self.view = place, links, axis, view
        self.first, self.second = first, second
        self.me = place.coord[axis]

    def block(self, shift):
        return self.place.blocks[self.axis][shift]

    def start(self):
        right, left = self.place.peer(self.axis, 1), self.place.peer(self.axis, 3)
        send = self.links.send
        self.far = [
            send(self.view(self.block(2), 0), self.first.at[0], right),
            send(self.view(self.block(2), 1), self.first.at[1], left),
        ]
        self.near = [
            send(self.view(self.block(1), 1), self.second.at[0, 1], right),
            send(self.view(self.block(3), 0), self.second.at[1, 0], left),
        ]

    def pass_on(self):
        right, left = self.place.peer(self.axis, 1), self.place.peer(self.axis, 3)
        for half, shift, device in ((0, 1, right), (1, 3, left)):
            self.far[half].wait_recv()
            own = self.view(self.block(shift), half)
            own[...] = (own[...].astype(F32) + self.first[half].astype(F32)).astype(BF16)
            self.near.append(self.links.send(own, self.second.at[half, half], device))

    def total(self, half):
        if half == 0:
            for copy in self.near:
                copy.wait_recv()
        own = self.view(self.block(0), half)[...].astype(F32)
        return own + self.second[0, half].astype(F32) + self.second[1, half].astype(F32)


class Plane:
    def __init__(self, place, links, axes, src, got):
        first, second = axes
        here = (place.coord[first], place.coord[second])
        self.copies = []
        for shift in (2, 1, 3, 0):
            for other in (2, 1, 3, 0):
                if shift or other:
                    there = src.at[place.blocks[first][shift], place.blocks[second][other]]
                    device = place.diagonal(first, shift, second, other)
                    self.copies.append(links.send(there, got.at[here[0], here[1]], device))
        got[here[0], here[1]] = src[here[0], here[1]]

    def wait(self):
        for copy in self.copies:
            copy.wait_recv()


def halves_of(ref, axis_dim, half_dim):
    extent = ref.shape[half_dim] // 2

    def view(block, half):
        index = [slice(None)] * len(ref.shape)
        index[half_dim] = pl.ds(half * extent, extent)
        index[axis_dim] = block
        return ref.at[tuple(index)]

    return view


def in_rows(extent, step, body, carry=0):
    def one(i, carry):
        return body(pl.multiple_of(i * step, step), carry)

    return lax.fori_loop(0, extent // step, one, carry)


def mean_square(values):
    return jnp.mean(values * values, axis=-1, keepdims=True)


def block_kernel(
    hin, gain1, w_in, w_conv, w_out, gain2, w_gate, w_up, w_down, cot,
    block_out, input_grad, gate_out, up_out, down_out, in_out, out_out, small_out,
    win, wout, n1, n1t, n2, n2t, hidt, gatet, upt, proj, gbuf, cv, mixed, mixedt, mid, mlow, cgbuf, mxg, pg,
    small, xb, xf, xn, xh,
    n2x, n2y, cotz, gx, uy, hz,
    g1a, g1b, g3, u1a, u1b, u3, d1a, d1b, d3,
    ia1, ia2, ib1, ib2, i3, ja1, ja2, jb1, jb2, j3, ka1, ka2, kb1, kb2, k3, oa1, oa2, ob1, ob2, o3,
    sm1, sm2,
    send_sem, recv_sem, load_sem,
):
    place = Place()
    links = Links(send_sem, recv_sem)
    head = place.head
    barrier = pltpu.get_barrier_semaphore()
    peers = [place.peer(axis, shift) for axis in "zxy" for shift in (1, 2, 3)]
    for first, second in ("zx", "xy"):
        peers += [place.diagonal(first, i, second, j) for i in (1, 2, 3) for j in (1, 2, 3)]
    peers += [place.sibling(), place.along[1], place.along[-1]]
    carried = jnp.where(lax.rem(place.seq, 16) != 0, 1.0, 0.0).astype(F32)
    carried_on = jnp.where(lax.rem(place.seq, 16) != 15, 1.0, 0.0).astype(F32)
    gathered = {}
    traded = {}
    shared = {}

    for axis, src, dst in (("z", cot, cotz), ("x", n2t, n2x), ("y", n2t, n2y)):
        part = src.shape[0] // 2
        mine = pl.ds(part * head, part)
        for shift in (1, 3, 2) if axis == "z" else (1, 3):
            gathered[axis, shift] = links.plan(
                src.at[mine], dst.at[shift - 1, mine], place.peer(axis, shift)
            )
        if axis != "z":
            for shift, here in ((1, 2 * head), (3, 2 * head + 1)):
                gathered[axis, 2, shift] = links.plan(
                    dst.at[shift - 1, here], dst.at[1, here], place.peer(axis, shift)
                )

    def gather(axis):
        for shift in (1, 3, 2) if axis == "z" else (1, 3):
            gathered[axis, shift].start()

    def relay(axis):
        for shift in (1, 3):
            gathered[axis, shift].wait_recv()
            gathered[axis, 2, shift].start()

    def trade(axis, src, dst):
        for shift in (1, 3, 2):
            block = place.blocks[axis][shift]
            rows = pl.ds(pl.multiple_of(block * 576, 576), 576)
            traded[axis, shift] = links.send(src.at[rows], dst.at[shift - 1], place.peer(axis, shift))

    def share(axis, dst):
        for shift in (1, 3, 2):
            if axis == "z":
                gathered[axis, shift].wait_recv()
            elif shift == 2:
                gathered[axis, 2, 1].wait_recv()
                gathered[axis, 2, 3].wait_recv()
            part = dst.shape[1] // 2
            here = dst.at[shift - 1, pl.ds(part * head, part)]
            shared[axis, shift] = links.send(here, here, place.sibling())

    taps = w_conv[...]

    def shifted_gated(r):
        window = gbuf[pl.ds(r, 48), :].astype(F32)
        return [pltpu.roll(window, 2, 0)[16:], pltpu.roll(window, 1, 0)[16:], window[16:]]

    def forward(wg, wu, wd, pre_g, pre_u, grad_h, hid_s, gg_s, ug_s, ffn_acc, n2g_acc):
        loads = []
        for src, dst in (
            (w_in.at[0], win.at[0]), (w_in.at[1], win.at[1]), (w_in.at[2], win.at[2]),
            (w_out, wout), (w_gate, wg), (w_up, wu), (w_down, wd),
        ):
            loads.append(pltpu.make_async_copy(src, dst, load_sem.at[len(loads)]))
        for copy in loads[:4]:
            copy.start()
        for device in peers:
            pl.semaphore_signal(barrier, inc=1, device_id=device, device_id_type=MESH)

        def norm_one(r, carry):
            x = hin[pl.ds(r, 32), :].astype(F32)
            n1[pl.ds(r, 32), :] = (x * lax.rsqrt(mean_square(x) + EPS) * gain1[...]).astype(BF16)
            return carry

        in_rows(256, 32, norm_one)
        pl.semaphore_wait(barrier, len(peers))
        gather("z")
        for part in (0, 2, 1):
            loads[part].wait()
            if part == 2:
                for copy in loads[4:]:
                    copy.start()
            proj[part] = jnp.dot(n1[...], win[part], preferred_element_type=F32)
            if part == 2:
                def gate_rows(r, carry):
                    here = pl.ds(r, 32)
                    gbuf[pl.ds(r + 16, 32), :] = (proj[0, here, :] * proj[2, here, :]).astype(BF16)
                    return carry

                in_rows(256, 32, gate_rows)
                edge = links.send(gbuf.at[pl.ds(256, 16)], gbuf.at[pl.ds(0, 16)], place.along[1])
        for i in range(4):
            n1t[i] = n1[:, 256 * i:256 * i + 256].T
        loads[3].wait()
        edge.wait_recv()
        gbuf[pl.ds(0, 16), :] = (gbuf[pl.ds(0, 16), :].astype(F32) * carried).astype(BF16)

        def mix_rows(r, carry):
            here = pl.ds(r, 32)
            old, last, now = shifted_gated(r)
            value = taps[0:1] * old + taps[1:2] * last + taps[2:3] * now
            cv[here, :] = value
            mixed[here, :] = (proj[1, here, :] * value).astype(BF16)
            return carry

        in_rows(256, 32, mix_rows)
        branch = []
        for half in range(2):
            here = pl.ds(128 * half, 128)
            xb[0, here, :] = jnp.dot(mixed[here, :], wout[...], preferred_element_type=F32).astype(BF16)
            branch.append(links.send(xb.at[0, here], xb.at[1, here], place.sibling()))
        for i in range(4):
            mixedt[i] = mixed[:, 128 * i:128 * i + 128].T

        def norm_two(r, carry):
            here = pl.ds(r, 32)
            middle = hin[here, :].astype(F32) + (xb[0, here, :].astype(F32) + xb[1, here, :].astype(F32))
            mid[here, :] = middle
            n2[here, :] = (middle * lax.rsqrt(mean_square(middle) + EPS) * gain2[...]).astype(BF16)
            return carry

        for half in range(2):
            branch[half].wait_recv()
            in_rows(128, 32, lambda r, carry: norm_two(r + 128 * half, carry))
        for i in range(4):
            n2t[i] = n2[:, 256 * i:256 * i + 256].T
        gather("x")
        gather("y")
        for copy in loads[4:]:
            copy.wait()
        cot_here = cot[...].reshape(256, 1024)
        for t in range(0, 2304, TILE):
            cut = slice(t, t + TILE)
            pre_g[...] = jnp.dot(n2[...], wg[:, cut], preferred_element_type=F32)
            pre_u[...] = jnp.dot(n2[...], wu[:, cut], preferred_element_type=F32)
            grad_h[...] = lax.dot_general(cot_here, wd[cut, :], NT, preferred_element_type=F32)
            if t + TILE == 2304:
                relay("x")
                relay("y")

            def act_rows(r, carry):
                here = pl.ds(r, 32)
                gate, up, grad = pre_g[here, :], pre_u[here, :], grad_h[here, :]
                sig = jax.nn.sigmoid(gate)
                act = gate * sig
                hid_s[here, :] = (act * up).astype(BF16)
                gg_s[here, :] = (grad * up * (sig * (1.0 + gate * (1.0 - sig)))).astype(BF16)
                ug_s[here, :] = (grad * act).astype(BF16)
                return carry

            in_rows(256, 32, act_rows)
            hidt[cut, :] = hid_s[...].T
            gatet[cut, :] = gg_s[...].T
            upt[cut, :] = ug_s[...].T
            ffn = jnp.dot(hid_s[...], wd[cut, :], preferred_element_type=F32)
            back = lax.dot_general(gg_s[...], wg[:, cut], NT, preferred_element_type=F32)
            back += lax.dot_general(ug_s[...], wu[:, cut], NT, preferred_element_type=F32)
            last = t + TILE == 2304
            if t > 0:
                ffn += ffn_acc[...]
                back += n2g_acc[...]
            if last:
                xn[0] = back.astype(BF16)
                xf[0] = ffn.astype(BF16)
            else:
                ffn_acc[...] = ffn
                n2g_acc[...] = back
        links.close()

    v = lambda *shape: pltpu.VMEM(shape, BF16)
    f = lambda *shape: pltpu.VMEM(shape, F32)
    pl.run_scoped(
        forward, v(1024, 2304), v(1024, 2304), v(2304, 1024),
        f(256, TILE), f(256, TILE), f(256, TILE), v(256, TILE), v(256, TILE), v(256, TILE),
        f(256, 1024), f(256, 1024),
    )

    def backward(g1, g2, u1, u2, d1, dt, d2, ia, ib, ic, ja, jb, jc, ka, kb, kc, oa, ob, oc):
        back_link = links.send(xn.at[0], xn.at[1], place.sibling())
        trade("z", hidt, hz)
        trade("x", gatet, gx)
        trade("y", upt, uy)
        ffn_link = links.send(xf.at[0], xf.at[1], place.sibling())
        share("z", cotz)
        back_link.wait_recv()
        ffn_link.wait_recv()
        small[...] = jnp.zeros((8, 1024), F32)

        def norm_two_back(i, total):
            here = pl.ds(pl.multiple_of(i * 32, 32), 32)
            grad = xn[0, here, :].astype(F32) + xn[1, here, :].astype(F32)
            middle = mid[here, :]
            ffn = xf[0, here, :].astype(F32) + xf[1, here, :].astype(F32)
            block_out[here, :] = (middle + ffn).astype(BF16)
            scale = lax.rsqrt(mean_square(middle) + EPS)
            unit = middle * scale
            total += jnp.sum((grad * unit).reshape(4, 8, 1024), axis=0)
            inner = grad * gain2[...]
            inner = scale * (inner - unit * jnp.mean(inner * unit, axis=-1, keepdims=True))
            middle = cot[i].astype(F32) + inner
            mid[here, :] = middle
            mlow[here, :] = middle.astype(BF16)
            return total

        total = lax.fori_loop(0, 8, norm_two_back, jnp.zeros((8, 1024), F32))
        small[1:2, :] = jnp.sum(total, axis=0, keepdims=True)
        mxg[...] = lax.dot_general(mlow[...], wout[...], NT, preferred_element_type=F32)

        def conv_back(r, totals):
            here = pl.ds(r, 32)
            grad = mxg[here, :]
            back = grad * proj[1, here, :]
            cgbuf[here, :] = back
            pg[here, 512:1024] = (grad * cv[here, :]).astype(BF16)
            return tuple(
                t + jnp.sum((back * g).reshape(4, 8, 512), axis=0) for t, g in zip(totals, shifted_gated(r))
            )

        totals = in_rows(256, 32, conv_back, (jnp.zeros((8, 512), F32),) * 3)
        edge = links.send(cgbuf.at[pl.ds(0, 8)], cgbuf.at[pl.ds(256, 8)], place.along[-1])
        for k in range(3):
            small[2 + k:3 + k, 0:512] = jnp.sum(totals[k], axis=0, keepdims=True)

        def out_tile(i, carry):
            res = jnp.dot(mixedt[i], mlow[...], preferred_element_type=F32)
            oa[i] = res.astype(BF16).reshape(8, 16, 1024)
            return carry

        lax.fori_loop(0, 4, out_tile, 0)
        out_ring = Ring(place, links, "z", halves_of(oa, 0, 1), oa1, oa2)
        out_ring.start()
        edge.wait_recv()
        cgbuf[pl.ds(256, 8), :] = cgbuf[pl.ds(256, 8), :] * carried_on

        def taps_back(r, carry):
            here = pl.ds(r, 32)
            window = cgbuf[pl.ds(r, 40), :]
            grad = (
                taps[2:3] * window[:32]
                + taps[1:2] * pltpu.roll(window, 39, 0)[:32]
                + taps[0:1] * pltpu.roll(window, 38, 0)[:32]
            )
            pg[here, 0:512] = (grad * proj[2, here, :]).astype(BF16)
            pg[here, 1024:1536] = (grad * proj[0, here, :]).astype(BF16)
            return carry

        in_rows(256, 32, taps_back)
        part = lax.dot_general(pg[:, 0:512], win[0], NT, preferred_element_type=F32)
        part += lax.dot_general(pg[:, 512:1024], win[1], NT, preferred_element_type=F32)
        part += lax.dot_general(pg[:, 1024:1536], win[2], NT, preferred_element_type=F32)
        xh[0] = part.astype(BF16)
        first_link = links.send(xh.at[0], xh.at[1], place.sibling())

        in_rings = [
            Ring(place, links, "z", lambda b, h: ia.at[b, pl.ds(2 * h, 2)], ia1, ia2),
            Ring(place, links, "x", lambda b, h: ja.at[pl.ds(2 * h, 2), b], ja1, ja2),
            Ring(place, links, "y", lambda b, h: ka.at[pl.ds(2 * h, 2), :, b], ka1, ka2),
        ]
        for part, own in enumerate((ia, ja, ka)):
            def in_tile(i, carry, own=own, left=CUTS[part], right=CUTS[part + 1]):
                res = jnp.dot(n1t[i], pg[:, left:right], preferred_element_type=F32)
                own[i] = res.astype(BF16).reshape(4, 4, 16, right - left)
                return carry

            lax.fori_loop(0, 4, in_tile, 0)
            in_rings[part].start()

        def ready(axis):
            for shift in (1, 3, 2):
                shared[axis, shift].wait_recv()
                traded[axis, shift].wait_recv()

        share("x", n2x)
        share("y", n2y)
        first_link.wait_recv()

        def norm_one_back(r, total):
            here = pl.ds(r, 32)
            grad = xh[0, here, :].astype(F32) + xh[1, here, :].astype(F32)
            x = hin[here, :].astype(F32)
            scale = lax.rsqrt(mean_square(x) + EPS)
            unit = x * scale
            total += jnp.sum((grad * unit).reshape(4, 8, 1024), axis=0)
            inner = grad * gain1[...]
            inner = scale * (inner - unit * jnp.mean(inner * unit, axis=-1, keepdims=True))
            input_grad[here, :] = (mid[here, :] + inner).astype(BF16)
            return total

        total = in_rows(256, 32, norm_one_back, jnp.zeros((8, 1024), F32))
        small[0:1, :] = jnp.sum(total, axis=0, keepdims=True)
        small_links = [links.send(small, sm1.at[0, shift - 1], place.peer("z", shift)) for shift in (1, 3, 2)]

        def wide(own_x, got_x, own_g, got_g, me, store):
            def tile(i, carry):
                own = own_g[pl.ds(pl.multiple_of(me * 576, 576), 576), :]
                res = lax.dot_general(own_x[i], own, NT, preferred_element_type=F32)
                for d in range(3):
                    res += lax.dot_general(got_x[d, i], got_g[d], NT, preferred_element_type=F32)
                store(i, res.astype(BF16))
                return carry

            lax.fori_loop(0, 4, tile, 0)

        ready("z")

        def down_tile(i, carry):
            own = hidt[pl.ds(pl.multiple_of(place.coord["z"] * 576 + i * 144, 144), 144), :]
            res = jnp.dot(own, cot[...].reshape(256, 1024), preferred_element_type=F32)
            for d in range(3):
                got = hz[d, pl.ds(pl.multiple_of(i * 144, 144), 144), :]
                res += jnp.dot(got, cotz[d].reshape(256, 1024), preferred_element_type=F32)
            d1[i] = res.astype(BF16).reshape(9, 16, 1024)
            return carry

        lax.fori_loop(0, 4, down_tile, 0)
        down_ring = Ring(place, links, "x", halves_of(d1, 0, 3), d1a, d1b)
        down_ring.start()

        for ring in in_rings:
            ring.pass_on()
        out_ring.pass_on()

        ready("x")

        def gate_store(i, res):
            g1[pl.ds(4 * i, 4)] = res.reshape(4, 4, 16, 576)

        wide(n2t, n2x, gatet, gx, place.coord["x"], gate_store)
        gate_ring = Ring(place, links, "y", halves_of(g1, 1, 0), g1a, g1b)
        gate_ring.start()

        ready("y")

        def up_store(i, res):
            u1[i] = res.reshape(16, 16, 576)

        wide(n2t, n2y, upt, uy, place.coord["y"], up_store)
        up_ring = Ring(place, links, "z", halves_of(u1, 0, 1), u1a, u1b)
        up_ring.start()

        for copy in small_links:
            copy.wait_recv()
        sm2[0] = small[...] + sm1[0, 0] + sm1[0, 1] + sm1[0, 2]
        small_links = [links.send(sm2.at[0], sm1.at[1, shift - 1], place.peer("x", shift)) for shift in (1, 3, 2)]
        down_ring.pass_on()

        gate_ring.pass_on()
        up_ring.pass_on()
        for ring, own in zip(in_rings, (ib, jb, kb)):
            for half in range(2):
                own[pl.ds(2 * half, 2)] = ring.total(half).astype(BF16)
        for half in range(2):
            res = out_ring.total(half).reshape(2, 4, 8, 1024)
            res = jnp.concatenate([res[..., :512], res[..., 512:]], axis=2)
            ob[pl.ds(2 * half, 2)] = res.astype(BF16)
        in_rings = [
            Ring(place, links, "x", halves_of(ib, 0, 1), ib1, ib2),
            Ring(place, links, "y", halves_of(jb, 1, 0), jb1, jb2),
            Ring(place, links, "z", halves_of(kb, 0, 1), kb1, kb2),
            Ring(place, links, "x", halves_of(ob, 0, 1), ob1, ob2),
        ]
        for ring in in_rings:
            ring.start()
        for copy in small_links:
            copy.wait_recv()
        sm2[1] = sm2[0] + sm1[1, 0] + sm1[1, 1] + sm1[1, 2]
        small_links = [links.send(sm2.at[1], sm1.at[2, shift - 1], place.peer("y", shift)) for shift in (1, 3, 2)]

        dt[pl.ds(144, 16), :] = jnp.zeros((16, 1024), F32)
        for half in range(2):
            dt[pl.ds(0, 144), half * 512:(half + 1) * 512] = down_ring.total(half).reshape(144, 512)
        for y in range(4):
            d2[y] = dt[pl.ds(36 * y, 48), :].astype(BF16)
        down_links = [
            links.send(d2.at[place.blocks["y"][shift]], d3.at[shift - 1], place.peer("y", shift))
            for shift in (2, 1, 3)
        ]
        for half in range(2):
            g2[pl.ds(2 * half, 2)] = gate_ring.total(half).astype(BF16).reshape(2, 4, 16, 576)
        gate_plane = Plane(place, links, "zx", g2, g3)
        for half in range(2):
            u2[pl.ds(2 * half, 2)] = up_ring.total(half).astype(BF16).reshape(2, 4, 16, 576)
        up_plane = Plane(place, links, "xy", u2, u3)

        for ring in in_rings:
            ring.pass_on()
        for copy in small_links:
            copy.wait_recv()
        small_out[...] = sm2[1] + sm1[2, 0] + sm1[2, 1] + sm1[2, 2]
        in_links = []
        lines = (("y", ic, i3), ("z", jc, j3), ("x", kc, k3), ("y", oc, o3))
        for ring, (axis, own, got) in zip(in_rings, lines):
            for half in range(2):
                own[pl.ds(2 * half, 2)] = ring.total(half).astype(BF16)
            for shift in (2, 1, 3):
                there = own.at[place.blocks[axis][shift]]
                in_links.append(links.send(there, got.at[shift - 1], place.peer(axis, shift)))
        for copy in down_links:
            copy.wait_recv()
        res = d2[place.coord["y"]].astype(F32)
        for d in range(3):
            res += d3[d].astype(F32)
        down_out[...] = res[:36]
        gate_plane.wait()
        gate_out[...] = jnp.concatenate([jnp.sum(g3[:, x].astype(F32), axis=0) for x in range(4)], axis=1)
        up_plane.wait()
        up_out[...] = jnp.concatenate([jnp.sum(u3[:, y].astype(F32), axis=0) for y in range(4)], axis=1)
        for copy in in_links:
            copy.wait_recv()
        sums = []
        for axis, own, got in lines:
            res = own[place.coord[axis]].astype(F32)
            for d in range(3):
                res += got[d].astype(F32)
            sums.append(res)
        res = jnp.concatenate(sums[:3], axis=1)
        for part in range(3):
            in_out[part] = res[:, 512 * part:512 * part + 512]
        out_out[:, 0:512] = sums[3][:8]
        out_out[:, 512:1024] = sums[3][8:]
        links.close()
        for copy in gathered.values():
            copy.wait_send()

    pl.run_scoped(
        backward,
        v(16, 4, 16, 576), v(4, 4, 16, 576), v(4, 16, 16, 576), v(4, 4, 16, 576),
        v(4, 9, 16, 1024), f(160, 1024), v(4, 48, 1024),
        *[v(*([4] * dims), 16, width) for width in (256, 640, 640) for dims in (3, 2, 1)],
        v(4, 8, 16, 1024), v(4, 4, 16, 512), v(4, 16, 512),
    )


def finish_kernel(
    block_in, grad_in, gate_in, up_in, down_in, in_in, out_in, small_in,
    block_out, input_grad, gate_out, up_out, down_out, in_out, out_out, gain1_out, gain2_out, conv_out,
):
    place = lax.axis_index("seq")
    for src, dst in (
        (block_in, block_out), (grad_in, input_grad), (gate_in, gate_out), (up_in, up_out),
        (down_in, down_out), (in_in, in_out), (out_in, out_out),
    ):
        dst[...] = src[...]
    gains = pltpu.roll(small_in[...], 1024 - 16 * place, 1)
    gain1_out[...] = gains[0:1, 0:16]
    gain2_out[...] = gains[1:2, 0:16]
    taps = pltpu.roll(small_in[...], 1024 - 8 * place, 1)
    conv_out[...] = taps[2:5, 0:8]


def shards(
    hidden_in, norm1_gain, in_weight, conv_weight, out_weight, norm2_gain, gate_weight, up_weight, down_weight,
    cotangent,
):
    v = lambda *shape: pltpu.VMEM(shape, BF16)
    f = lambda *shape: pltpu.VMEM(shape, F32)

    def ring(*half):
        return [v(2, *half), v(2, 2, *half)]

    scratch = [
        v(3, 1024, 512), v(512, 1024), v(256, 1024), v(4, 256, 256), v(256, 1024), v(4, 256, 256),
        v(2304, 256), v(2304, 256), v(2304, 256), f(3, 256, 512), v(272, 512), f(256, 512), v(256, 512),
        v(4, 128, 256), f(256, 1024), v(256, 1024), f(264, 512), f(256, 512), v(256, 1536), f(8, 1024),
        *[v(2, 256, 1024)] * 4,
        v(3, 4, 256, 256), v(3, 4, 256, 256), v(3, 8, 32, 1024),
        v(3, 576, 256), v(3, 576, 256), v(3, 576, 256),
        *ring(8, 16, 576), v(4, 4, 16, 576), *ring(8, 16, 576), v(4, 4, 16, 576), *ring(9, 16, 512), v(3, 48, 1024),
        *[
            buffer
            for width in (256, 640, 640)
            for buffer in (*ring(2, 4, 16, width), *ring(2, 16, width), v(3, 16, width))
        ],
        *ring(4, 16, 1024), *ring(2, 16, 512), v(3, 16, 512),
        f(3, 3, 8, 1024), f(2, 8, 1024),
        pltpu.SemaphoreType.DMA((N_SEMS,)), pltpu.SemaphoreType.DMA((N_SEMS,)), pltpu.SemaphoreType.DMA((7,)),
    ]
    vmem = pl.BlockSpec(memory_space=pltpu.VMEM)
    far = pl.BlockSpec(memory_space=pl.ANY)
    (
        block_out, input_grad, gate_final, up_final, down_final, in_final, out_final, small_final,
    ) = pl.pallas_call(
        block_kernel,
        out_shape=[jax.ShapeDtypeStruct((256, 1024), BF16)] * 2
        + [
            jax.ShapeDtypeStruct(shape, F32)
            for shape in ((16, 2304), (16, 2304), (36, 1024), (3, 16, 512), (8, 1024), (8, 1024))
        ],
        in_specs=[vmem, vmem, far, vmem, far, vmem, far, far, far, vmem],
        out_specs=[vmem] * 8,
        scratch_shapes=scratch,
        compiler_params=pltpu.CompilerParams(
            collective_id=0, has_side_effects=True, vmem_limit_bytes=62 * 2**20
        ),
        name="block",
    )(
        hidden_in, norm1_gain.reshape(1, 1024), in_weight.transpose(1, 0, 2), conv_weight.T, out_weight,
        norm2_gain.reshape(1, 1024), gate_weight, up_weight, down_weight, cotangent.reshape(8, 32, 1024),
    )
    (
        block_out, input_grad, gate_final, up_final, down_final, in_final, out_final, gain1_final, gain2_final,
        conv_final,
    ) = pl.pallas_call(
        finish_kernel,
        out_shape=[jax.ShapeDtypeStruct((256, 1024), BF16)] * 2
        + [
            jax.ShapeDtypeStruct(shape, F32)
            for shape in (
                (16, 2304), (16, 2304), (36, 1024), (3, 16, 512), (8, 1024), (1, 16), (1, 16), (3, 8),
            )
        ],
        in_specs=[vmem] * 8,
        out_specs=[vmem] * 10,
        name="finish",
    )(block_out, input_grad, gate_final, up_final, down_final, in_final, out_final, small_final)
    return (
        block_out,
        input_grad,
        gain1_final.reshape(16),
        in_final.transpose(1, 0, 2),
        conv_final.T,
        out_final,
        gain2_final.reshape(16),
        gate_final,
        up_final,
        down_final,
    )


def solution(mesh):
    placed = (
        P("seq", None),
        P(),
        P(None, None, "head"),
        P("head", None),
        P("head", None),
        P(),
        P(None, "head"),
        P(None, "head"),
        P("head", None),
        P("seq", None),
    )
    return jax.shard_map(
        shards,
        mesh=mesh,
        in_specs=placed,
        out_specs=(
            P("seq", None),
            P("seq", None),
            P("seq"),
            P("seq", None, "head"),
            P(("head", "seq"), None),
            P(("head", "seq"), None),
            P("seq"),
            P("seq", "head"),
            P("seq", "head"),
            P(("head", "seq"), None),
        ),
        check_vma=False,
    )
```

```python
import jax
import jax.numpy as jnp
from jax import lax
from jax.experimental import pallas as pl
from jax.experimental.pallas import tpu as pltpu
from jax.sharding import PartitionSpec as P

EPS = 1e-05
MESH = pl.DeviceIdType.MESH
F32 = jnp.float32
BF16 = jnp.bfloat16
NT = (((1,), (1,)), ((), ()))
N_SEMS = 210
TILE = 768
CUTS = (0, 256, 896, 1536)


class Place:
    def __init__(self):
        self.seq = lax.axis_index("seq")
        self.head = lax.axis_index("head")
        self.coord = {
            "z": lax.div(self.seq, 16),
            "x": lax.rem(lax.div(self.seq, 4), 4),
            "y": lax.rem(self.seq, 4),
        }

        self.blocks = {
            axis: [self.coord[axis]] + [lax.rem(self.coord[axis] + shift, 4) for shift in (1, 2, 3)]
            for axis in "zxy"
        }
        self.peers = {}
        for axis in "zxy":
            for shift in (1, 2, 3):
                moved = dict(self.coord)
                moved[axis] = self.blocks[axis][shift]
                self.peers[axis, shift] = ((moved["z"] * 4 + moved["x"]) * 4 + moved["y"], self.head)
        self.along = {
            shift: (lax.rem(self.seq + 64 + shift, 64), self.head) for shift in (1, -1)
        }

    def peer(self, axis, shift):
        return self.peers[axis, shift]

    def diagonal(self, first, shift, second, other):
        moved = dict(self.coord)
        moved[first] = self.blocks[first][shift]
        moved[second] = self.blocks[second][other]
        return ((moved["z"] * 4 + moved["x"]) * 4 + moved["y"], self.head)

    def sibling(self):
        return (self.seq, 1 - self.head)


class Links:
    def __init__(self, send_sem, recv_sem):
        self.send_sem = send_sem
        self.recv_sem = recv_sem
        self.used = 0
        self.open = []

    def plan(self, src, dst, device):
        copy = pltpu.make_async_remote_copy(
            src_ref=src,
            dst_ref=dst,
            send_sem=self.send_sem.at[self.used],
            recv_sem=self.recv_sem.at[self.used],
            device_id=device,
            device_id_type=MESH,
        )
        self.used += 1
        return copy

    def send(self, src, dst, device):
        copy = self.plan(src, dst, device)
        copy.start()
        self.open.append(copy)
        return copy

    def close(self):
        for copy in self.open:
            copy.wait_send()
        self.open = []


class Ring:
    def __init__(self, place, links, axis, view, first, second):
        self.place, self.links, self.axis, self.view = place, links, axis, view
        self.first, self.second = first, second
        self.me = place.coord[axis]

    def block(self, shift):
        return self.place.blocks[self.axis][shift]

    def start(self):
        right, left = self.place.peer(self.axis, 1), self.place.peer(self.axis, 3)
        send = self.links.send
        self.far = [
            send(self.view(self.block(2), 0), self.first.at[0], right),
            send(self.view(self.block(2), 1), self.first.at[1], left),
        ]
        self.near = [
            send(self.view(self.block(1), 1), self.second.at[0, 1], right),
            send(self.view(self.block(3), 0), self.second.at[1, 0], left),
        ]

    def pass_on(self):
        right, left = self.place.peer(self.axis, 1), self.place.peer(self.axis, 3)
        for half, shift, device in ((0, 1, right), (1, 3, left)):
            self.far[half].wait_recv()
            own = self.view(self.block(shift), half)
            own[...] = (own[...].astype(F32) + self.first[half].astype(F32)).astype(BF16)
            self.near.append(self.links.send(own, self.second.at[half, half], device))

    def total(self, half):
        if half == 0:
            for copy in self.near:
                copy.wait_recv()
        own = self.view(self.block(0), half)[...].astype(F32)
        return own + self.second[0, half].astype(F32) + self.second[1, half].astype(F32)


class Plane:
    def __init__(self, place, links, axes, src, got):
        first, second = axes
        here = (place.coord[first], place.coord[second])
        self.copies = []
        for shift in (2, 1, 3, 0):
            for other in (2, 1, 3, 0):
                if shift or other:
                    there = src.at[place.blocks[first][shift], place.blocks[second][other]]
                    device = place.diagonal(first, shift, second, other)
                    self.copies.append(links.send(there, got.at[here[0], here[1]], device))
        got[here[0], here[1]] = src[here[0], here[1]]

    def wait(self):
        for copy in self.copies:
            copy.wait_recv()


def halves_of(ref, axis_dim, half_dim):
    extent = ref.shape[half_dim] // 2

    def view(block, half):
        index = [slice(None)] * len(ref.shape)
        index[half_dim] = pl.ds(half * extent, extent)
        index[axis_dim] = block
        return ref.at[tuple(index)]

    return view


def in_rows(extent, step, body, carry=0):
    def one(i, carry):
        return body(pl.multiple_of(i * step, step), carry)

    return lax.fori_loop(0, extent // step, one, carry)


def mean_square(values):
    return jnp.mean(values * values, axis=-1, keepdims=True)


def block_kernel(
    hin, gain1, w_in, w_conv, w_out, gain2, w_gate, w_up, w_down, cot,
    block_out, input_grad, gate_out, up_out, down_out, in_out, out_out, small_out,
    win, wout, n1, n1t, n2, n2t, hidt, gatet, upt, proj, gbuf, cv, mixed, mixedt, mid, mlow, cgbuf, mxg, pg,
    small, xb, xf, xn, xh,
    n2x, n2y, cotz, gx, uy, hz,
    g1a, g1b, g3, u1a, u1b, u3, d1a, d1b, d3,
    ia1, ia2, ib1, ib2, i3, ja1, ja2, jb1, jb2, j3, ka1, ka2, kb1, kb2, k3, oa1, oa2, ob1, ob2, o3,
    sm1, sm2,
    send_sem, recv_sem, load_sem,
):
    place = Place()
    links = Links(send_sem, recv_sem)
    head = place.head
    barrier = pltpu.get_barrier_semaphore()
    peers = [place.peer(axis, shift) for axis in "zxy" for shift in (1, 2, 3)]
    for first, second in ("zx", "xy"):
        peers += [place.diagonal(first, i, second, j) for i in (1, 2, 3) for j in (1, 2, 3)]
    peers += [place.sibling(), place.along[1], place.along[-1]]
    carried = jnp.where(lax.rem(place.seq, 16) != 0, 1.0, 0.0).astype(F32)
    carried_on = jnp.where(lax.rem(place.seq, 16) != 15, 1.0, 0.0).astype(F32)
    gathered = {}
    traded = {}
    shared = {}

    for axis, src, dst in (("z", cot, cotz), ("x", n2t, n2x), ("y", n2t, n2y)):
        part = src.shape[0] // 2
        mine = pl.ds(part * head, part)
        for shift in (1, 3, 2) if axis == "z" else (1, 3):
            gathered[axis, shift] = links.plan(
                src.at[mine], dst.at[shift - 1, mine], place.peer(axis, shift)
            )
        if axis != "z":
            for shift, here in ((1, 2 * head), (3, 2 * head + 1)):
                gathered[axis, 2, shift] = links.plan(
                    dst.at[shift - 1, here], dst.at[1, here], place.peer(axis, shift)
                )

    def gather(axis):
        for shift in (1, 3, 2) if axis == "z" else (1, 3):
            gathered[axis, shift].start()

    def relay(axis):
        for shift in (1, 3):
            gathered[axis, shift].wait_recv()
            gathered[axis, 2, shift].start()

    for axis, src, dst in (("z", hidt, hz), ("x", gatet, gx), ("y", upt, uy)):
        for shift in (1, 3, 2):
            rows = pl.ds(pl.multiple_of(place.blocks[axis][shift] * 576, 576), 576)
            traded[axis, shift] = links.plan(src.at[rows], dst.at[shift - 1], place.peer(axis, shift))
    back_link = links.plan(xn.at[0], xn.at[1], place.sibling())
    ffn_link = links.plan(xf.at[0], xf.at[1], place.sibling())

    def share(axis, dst):
        for shift in (1, 3, 2):
            if axis == "z":
                gathered[axis, shift].wait_recv()
            elif shift == 2:
                gathered[axis, 2, 1].wait_recv()
                gathered[axis, 2, 3].wait_recv()
            part = dst.shape[1] // 2
            here = dst.at[shift - 1, pl.ds(part * head, part)]
            shared[axis, shift] = links.send(here, here, place.sibling())

    taps = w_conv[...]

    def shifted_gated(r):
        window = gbuf[pl.ds(r, 48), :].astype(F32)
        return [pltpu.roll(window, 2, 0)[16:], pltpu.roll(window, 1, 0)[16:], window[16:]]

    def forward(wg, wu, wd, pre_g, pre_u, grad_h, hid_s, gg_s, ug_s, n2g_acc):
        loads = []
        for src, dst in (
            (w_in.at[0], win.at[0]), (w_in.at[1], win.at[1]), (w_in.at[2], win.at[2]),
            (w_out, wout), (w_down, wd), (w_gate, wg), (w_up, wu),
        ):
            loads.append(pltpu.make_async_copy(src, dst, load_sem.at[len(loads)]))
        for copy in loads[:4]:
            copy.start()
        for device in peers:
            pl.semaphore_signal(barrier, inc=1, device_id=device, device_id_type=MESH)

        def norm_one(r, carry):
            x = hin[pl.ds(r, 32), :].astype(F32)
            n1[pl.ds(r, 32), :] = (x * lax.rsqrt(mean_square(x) + EPS) * gain1[...]).astype(BF16)
            return carry

        in_rows(256, 32, norm_one)
        pl.semaphore_wait(barrier, len(peers))
        gather("z")
        for part in (0, 2, 1):
            loads[part].wait()
            if part == 2:
                for copy in loads[4:]:
                    copy.start()
            proj[part] = jnp.dot(n1[...], win[part], preferred_element_type=F32)
            if part == 2:
                def gate_rows(r, carry):
                    here = pl.ds(r, 32)
                    gbuf[pl.ds(r + 16, 32), :] = (proj[0, here, :] * proj[2, here, :]).astype(BF16)
                    return carry

                in_rows(256, 32, gate_rows)
                edge = links.send(gbuf.at[pl.ds(256, 16)], gbuf.at[pl.ds(0, 16)], place.along[1])
        for i in range(4):
            n1t[i] = n1[:, 256 * i:256 * i + 256].T
        loads[3].wait()
        loads[4].wait()

        def hidden_grad(tile):
            part = wd[tile * TILE:tile * TILE + TILE, :]
            grad_h[tile] = lax.dot_general(
                cot[...].reshape(256, 1024), part, NT, preferred_element_type=F32
            )

        hidden_grad(0)
        hidden_grad(1)
        edge.wait_recv()
        gbuf[pl.ds(0, 16), :] = (gbuf[pl.ds(0, 16), :].astype(F32) * carried).astype(BF16)

        def mix_rows(r, carry):
            here = pl.ds(r, 32)
            old, last, now = shifted_gated(r)
            value = taps[0:1] * old + taps[1:2] * last + taps[2:3] * now
            cv[here, :] = value
            mixed[here, :] = (proj[1, here, :] * value).astype(BF16)
            return carry

        in_rows(256, 32, mix_rows)
        branch = []
        for half in range(2):
            here = pl.ds(128 * half, 128)
            xb[0, here, :] = jnp.dot(mixed[here, :], wout[...], preferred_element_type=F32).astype(BF16)
            branch.append(links.send(xb.at[0, here], xb.at[1, here], place.sibling()))
        for i in range(4):
            mixedt[i] = mixed[:, 128 * i:128 * i + 128].T

        hidden_grad(2)

        def norm_two(r, carry):
            here = pl.ds(r, 32)
            middle = hin[here, :].astype(F32) + (xb[0, here, :].astype(F32) + xb[1, here, :].astype(F32))
            mid[here, :] = middle
            n2[here, :] = (middle * lax.rsqrt(mean_square(middle) + EPS) * gain2[...]).astype(BF16)
            return carry

        for half in range(2):
            branch[half].wait_recv()
            in_rows(128, 32, lambda r, carry: norm_two(r + 128 * half, carry))
        for i in range(4):
            n2t[i] = n2[:, 256 * i:256 * i + 256].T
        gather("x")
        gather("y")
        for copy in loads[5:]:
            copy.wait()
        for t in range(0, 2304, TILE):
            cut = slice(t, t + TILE)
            pre_g[...] = jnp.dot(n2[...], wg[:, cut], preferred_element_type=F32)
            pre_u[...] = jnp.dot(n2[...], wu[:, cut], preferred_element_type=F32)
            if t + TILE == 2304:
                relay("x")
                relay("y")

            def act_rows(r, carry, t=t):
                here = pl.ds(r, 32)
                gate, up, grad = pre_g[here, :], pre_u[here, :], grad_h[t // TILE, here, :]
                sig = jax.nn.sigmoid(gate)
                act = gate * sig
                hid_s[here, t:t + TILE] = (act * up).astype(BF16)
                gg_s[here, :] = (grad * up * (sig * (1.0 + gate * (1.0 - sig)))).astype(BF16)
                ug_s[here, :] = (grad * act).astype(BF16)
                return carry

            in_rows(256, 32, act_rows)
            hidt[cut, :] = hid_s[:, cut].T
            gatet[cut, :] = gg_s[...].T
            upt[cut, :] = ug_s[...].T
            last = t + TILE == 2304
            if last:
                for copy in traded.values():
                    copy.start()
            back = lax.dot_general(gg_s[...], wg[:, cut], NT, preferred_element_type=F32)
            back += lax.dot_general(ug_s[...], wu[:, cut], NT, preferred_element_type=F32)
            if t > 0:
                back += n2g_acc[...]
            if last:
                xn[0] = back.astype(BF16)
            else:
                n2g_acc[...] = back
        back_link.start()
        xf[0] = jnp.dot(hid_s[...], wd[...], preferred_element_type=F32).astype(BF16)
        ffn_link.start()
        links.close()

    v = lambda *shape: pltpu.VMEM(shape, BF16)
    f = lambda *shape: pltpu.VMEM(shape, F32)
    pl.run_scoped(
        forward, v(1024, 2304), v(1024, 2304), v(2304, 1024),
        f(256, TILE), f(256, TILE), f(3, 256, TILE), v(256, 2304), v(256, TILE), v(256, TILE),
        f(256, 1024),
    )

    def backward(g1, g2, u1, u2, d1, dt, d2, ia, ib, ic, ja, jb, jc, ka, kb, kc, oa, ob, oc):
        share("z", cotz)
        back_link.wait_recv()
        ffn_link.wait_recv()
        small[...] = jnp.zeros((8, 1024), F32)

        def norm_two_back(i, total):
            here = pl.ds(pl.multiple_of(i * 32, 32), 32)
            grad = xn[0, here, :].astype(F32) + xn[1, here, :].astype(F32)
            middle = mid[here, :]
            ffn = xf[0, here, :].astype(F32) + xf[1, here, :].astype(F32)
            block_out[here, :] = (middle + ffn).astype(BF16)
            scale = lax.rsqrt(mean_square(middle) + EPS)
            unit = middle * scale
            total += jnp.sum((grad * unit).reshape(4, 8, 1024), axis=0)
            inner = grad * gain2[...]
            inner = scale * (inner - unit * jnp.mean(inner * unit, axis=-1, keepdims=True))
            middle = cot[i].astype(F32) + inner
            mid[here, :] = middle
            mlow[here, :] = middle.astype(BF16)
            return total

        total = lax.fori_loop(0, 8, norm_two_back, jnp.zeros((8, 1024), F32))
        small[1:2, :] = jnp.sum(total, axis=0, keepdims=True)
        mxg[...] = lax.dot_general(mlow[...], wout[...], NT, preferred_element_type=F32)

        def conv_back(r, totals):
            here = pl.ds(r, 32)
            grad = mxg[here, :]
            back = grad * proj[1, here, :]
            cgbuf[here, :] = back
            pg[here, 512:1024] = (grad * cv[here, :]).astype(BF16)
            return tuple(
                t + jnp.sum((back * g).reshape(4, 8, 512), axis=0) for t, g in zip(totals, shifted_gated(r))
            )

        totals = in_rows(256, 32, conv_back, (jnp.zeros((8, 512), F32),) * 3)
        edge = links.send(cgbuf.at[pl.ds(0, 8)], cgbuf.at[pl.ds(256, 8)], place.along[-1])
        for k in range(3):
            small[2 + k:3 + k, 0:512] = jnp.sum(totals[k], axis=0, keepdims=True)

        def out_tile(i, carry):
            res = jnp.dot(mixedt[i], mlow[...], preferred_element_type=F32)
            oa[i] = res.astype(BF16).reshape(8, 16, 1024)
            return carry

        lax.fori_loop(0, 4, out_tile, 0)
        out_ring = Ring(place, links, "z", halves_of(oa, 0, 1), oa1, oa2)
        out_ring.start()
        edge.wait_recv()
        cgbuf[pl.ds(256, 8), :] = cgbuf[pl.ds(256, 8), :] * carried_on

        def taps_back(r, carry):
            here = pl.ds(r, 32)
            window = cgbuf[pl.ds(r, 40), :]
            grad = (
                taps[2:3] * window[:32]
                + taps[1:2] * pltpu.roll(window, 39, 0)[:32]
                + taps[0:1] * pltpu.roll(window, 38, 0)[:32]
            )
            pg[here, 0:512] = (grad * proj[2, here, :]).astype(BF16)
            pg[here, 1024:1536] = (grad * proj[0, here, :]).astype(BF16)
            return carry

        in_rows(256, 32, taps_back)
        part = lax.dot_general(pg[:, 0:512], win[0], NT, preferred_element_type=F32)
        part += lax.dot_general(pg[:, 512:1024], win[1], NT, preferred_element_type=F32)
        part += lax.dot_general(pg[:, 1024:1536], win[2], NT, preferred_element_type=F32)
        xh[0] = part.astype(BF16)
        first_link = links.send(xh.at[0], xh.at[1], place.sibling())

        in_rings = [
            Ring(place, links, "z", lambda b, h: ia.at[b, pl.ds(2 * h, 2)], ia1, ia2),
            Ring(place, links, "x", lambda b, h: ja.at[pl.ds(2 * h, 2), b], ja1, ja2),
            Ring(place, links, "y", lambda b, h: ka.at[pl.ds(2 * h, 2), :, b], ka1, ka2),
        ]
        for part, own in enumerate((ia, ja, ka)):
            def in_tile(i, carry, own=own, left=CUTS[part], right=CUTS[part + 1]):
                res = jnp.dot(n1t[i], pg[:, left:right], preferred_element_type=F32)
                own[i] = res.astype(BF16).reshape(4, 4, 16, right - left)
                return carry

            lax.fori_loop(0, 4, in_tile, 0)
            in_rings[part].start()

        def ready(axis):
            for shift in (1, 3, 2):
                shared[axis, shift].wait_recv()
                traded[axis, shift].wait_recv()

        share("x", n2x)
        share("y", n2y)
        first_link.wait_recv()

        def norm_one_back(r, total):
            here = pl.ds(r, 32)
            grad = xh[0, here, :].astype(F32) + xh[1, here, :].astype(F32)
            x = hin[here, :].astype(F32)
            scale = lax.rsqrt(mean_square(x) + EPS)
            unit = x * scale
            total += jnp.sum((grad * unit).reshape(4, 8, 1024), axis=0)
            inner = grad * gain1[...]
            inner = scale * (inner - unit * jnp.mean(inner * unit, axis=-1, keepdims=True))
            input_grad[here, :] = (mid[here, :] + inner).astype(BF16)
            return total

        total = in_rows(256, 32, norm_one_back, jnp.zeros((8, 1024), F32))
        small[0:1, :] = jnp.sum(total, axis=0, keepdims=True)
        small_links = [links.send(small, sm1.at[0, shift - 1], place.peer("z", shift)) for shift in (1, 3, 2)]

        def wide(own_x, got_x, own_g, got_g, me, store):
            def tile(i, carry):
                own = own_g[pl.ds(pl.multiple_of(me * 576, 576), 576), :]
                res = lax.dot_general(own_x[i], own, NT, preferred_element_type=F32)
                for d in range(3):
                    res += lax.dot_general(got_x[d, i], got_g[d], NT, preferred_element_type=F32)
                store(i, res.astype(BF16))
                return carry

            lax.fori_loop(0, 4, tile, 0)

        ready("z")

        def down_tile(i, carry):
            own = hidt[pl.ds(pl.multiple_of(place.coord["z"] * 576 + i * 144, 144), 144), :]
            res = jnp.dot(own, cot[...].reshape(256, 1024), preferred_element_type=F32)
            for d in range(3):
                got = hz[d, pl.ds(pl.multiple_of(i * 144, 144), 144), :]
                res += jnp.dot(got, cotz[d].reshape(256, 1024), preferred_element_type=F32)
            d1[i] = res.astype(BF16).reshape(9, 16, 1024)
            return carry

        lax.fori_loop(0, 4, down_tile, 0)
        down_ring = Ring(place, links, "x", halves_of(d1, 0, 3), d1a, d1b)
        down_ring.start()

        for ring in in_rings:
            ring.pass_on()
        out_ring.pass_on()

        ready("x")

        def gate_store(i, res):
            g1[pl.ds(4 * i, 4)] = res.reshape(4, 4, 16, 576)

        wide(n2t, n2x, gatet, gx, place.coord["x"], gate_store)
        gate_ring = Ring(place, links, "y", halves_of(g1, 1, 0), g1a, g1b)
        gate_ring.start()

        ready("y")

        def up_store(i, res):
            u1[i] = res.reshape(16, 16, 576)

        wide(n2t, n2y, upt, uy, place.coord["y"], up_store)
        up_ring = Ring(place, links, "z", halves_of(u1, 0, 1), u1a, u1b)
        up_ring.start()

        for copy in small_links:
            copy.wait_recv()
        sm2[0] = small[...] + sm1[0, 0] + sm1[0, 1] + sm1[0, 2]
        small_links = [links.send(sm2.at[0], sm1.at[1, shift - 1], place.peer("x", shift)) for shift in (1, 3, 2)]
        down_ring.pass_on()

        gate_ring.pass_on()
        up_ring.pass_on()
        for ring, own in zip(in_rings, (ib, jb, kb)):
            for half in range(2):
                own[pl.ds(2 * half, 2)] = ring.total(half).astype(BF16)
        for half in range(2):
            res = out_ring.total(half).reshape(2, 4, 8, 1024)
            res = jnp.concatenate([res[..., :512], res[..., 512:]], axis=2)
            ob[pl.ds(2 * half, 2)] = res.astype(BF16)
        in_rings = [
            Ring(place, links, "x", halves_of(ib, 0, 1), ib1, ib2),
            Ring(place, links, "y", halves_of(jb, 1, 0), jb1, jb2),
            Ring(place, links, "z", halves_of(kb, 0, 1), kb1, kb2),
            Ring(place, links, "x", halves_of(ob, 0, 1), ob1, ob2),
        ]
        for ring in in_rings:
            ring.start()
        for copy in small_links:
            copy.wait_recv()
        sm2[1] = sm2[0] + sm1[1, 0] + sm1[1, 1] + sm1[1, 2]
        small_links = [links.send(sm2.at[1], sm1.at[2, shift - 1], place.peer("y", shift)) for shift in (1, 3, 2)]

        for ring in in_rings:
            ring.pass_on()
        dt[pl.ds(144, 16), :] = jnp.zeros((16, 1024), F32)
        for half in range(2):
            dt[pl.ds(0, 144), half * 512:(half + 1) * 512] = down_ring.total(half).reshape(144, 512)
        for y in range(4):
            d2[y] = dt[pl.ds(36 * y, 48), :].astype(BF16)
        down_links = [
            links.send(d2.at[place.blocks["y"][shift]], d3.at[shift - 1], place.peer("y", shift))
            for shift in (2, 1, 3)
        ]
        for half in range(2):
            g2[pl.ds(2 * half, 2)] = gate_ring.total(half).astype(BF16).reshape(2, 4, 16, 576)
        gate_plane = Plane(place, links, "zx", g2, g3)
        in_links = []
        lines = (("y", ic, i3), ("z", jc, j3), ("x", kc, k3), ("y", oc, o3))
        for ring, (axis, own, got) in zip(in_rings, lines):
            for half in range(2):
                own[pl.ds(2 * half, 2)] = ring.total(half).astype(BF16)
            for shift in (2, 1, 3):
                there = own.at[place.blocks[axis][shift]]
                in_links.append(links.send(there, got.at[shift - 1], place.peer(axis, shift)))
        for half in range(2):
            u2[pl.ds(2 * half, 2)] = up_ring.total(half).astype(BF16).reshape(2, 4, 16, 576)
        up_plane = Plane(place, links, "xy", u2, u3)

        for copy in small_links:
            copy.wait_recv()
        small_out[...] = sm2[1] + sm1[2, 0] + sm1[2, 1] + sm1[2, 2]
        for copy in down_links:
            copy.wait_recv()
        res = d2[place.coord["y"]].astype(F32)
        for d in range(3):
            res += d3[d].astype(F32)
        down_out[...] = res[:36]
        gate_plane.wait()
        gate_out[...] = jnp.concatenate([jnp.sum(g3[:, x].astype(F32), axis=0) for x in range(4)], axis=1)
        up_plane.wait()
        up_out[...] = jnp.concatenate([jnp.sum(u3[:, y].astype(F32), axis=0) for y in range(4)], axis=1)
        for copy in in_links:
            copy.wait_recv()
        sums = []
        for axis, own, got in lines:
            res = own[place.coord[axis]].astype(F32)
            for d in range(3):
                res += got[d].astype(F32)
            sums.append(res)
        res = jnp.concatenate(sums[:3], axis=1)
        for part in range(3):
            in_out[part] = res[:, 512 * part:512 * part + 512]
        out_out[:, 0:512] = sums[3][:8]
        out_out[:, 512:1024] = sums[3][8:]
        links.close()
        for copy in (*gathered.values(), *traded.values(), back_link, ffn_link):
            copy.wait_send()

    pl.run_scoped(
        backward,
        v(16, 4, 16, 576), v(4, 4, 16, 576), v(4, 16, 16, 576), v(4, 4, 16, 576),
        v(4, 9, 16, 1024), f(160, 1024), v(4, 48, 1024),
        *[v(*([4] * dims), 16, width) for width in (256, 640, 640) for dims in (3, 2, 1)],
        v(4, 8, 16, 1024), v(4, 4, 16, 512), v(4, 16, 512),
    )


def finish_kernel(
    block_in, grad_in, gate_in, up_in, down_in, in_in, out_in, small_in,
    block_out, input_grad, gate_out, up_out, down_out, in_out, out_out, gain1_out, gain2_out, conv_out,
):
    place = lax.axis_index("seq")
    for src, dst in (
        (block_in, block_out), (grad_in, input_grad), (gate_in, gate_out), (up_in, up_out),
        (down_in, down_out), (in_in, in_out), (out_in, out_out),
    ):
        dst[...] = src[...]
    gains = pltpu.roll(small_in[...], 1024 - 16 * place, 1)
    gain1_out[...] = gains[0:1, 0:16]
    gain2_out[...] = gains[1:2, 0:16]
    taps = pltpu.roll(small_in[...], 1024 - 8 * place, 1)
    conv_out[...] = taps[2:5, 0:8]


def shards(
    hidden_in, norm1_gain, in_weight, conv_weight, out_weight, norm2_gain, gate_weight, up_weight, down_weight,
    cotangent,
):
    v = lambda *shape: pltpu.VMEM(shape, BF16)
    f = lambda *shape: pltpu.VMEM(shape, F32)

    def ring(*half):
        return [v(2, *half), v(2, 2, *half)]

    scratch = [
        v(3, 1024, 512), v(512, 1024), v(256, 1024), v(4, 256, 256), v(256, 1024), v(4, 256, 256),
        v(2304, 256), v(2304, 256), v(2304, 256), f(3, 256, 512), v(272, 512), f(256, 512), v(256, 512),
        v(4, 128, 256), f(256, 1024), v(256, 1024), f(264, 512), f(256, 512), v(256, 1536), f(8, 1024),
        *[v(2, 256, 1024)] * 4,
        v(3, 4, 256, 256), v(3, 4, 256, 256), v(3, 8, 32, 1024),
        v(3, 576, 256), v(3, 576, 256), v(3, 576, 256),
        *ring(8, 16, 576), v(4, 4, 16, 576), *ring(8, 16, 576), v(4, 4, 16, 576), *ring(9, 16, 512), v(3, 48, 1024),
        *[
            buffer
            for width in (256, 640, 640)
            for buffer in (*ring(2, 4, 16, width), *ring(2, 16, width), v(3, 16, width))
        ],
        *ring(4, 16, 1024), *ring(2, 16, 512), v(3, 16, 512),
        f(3, 3, 8, 1024), f(2, 8, 1024),
        pltpu.SemaphoreType.DMA((N_SEMS,)), pltpu.SemaphoreType.DMA((N_SEMS,)), pltpu.SemaphoreType.DMA((7,)),
    ]
    vmem = pl.BlockSpec(memory_space=pltpu.VMEM)
    far = pl.BlockSpec(memory_space=pl.ANY)
    (
        block_out, input_grad, gate_final, up_final, down_final, in_final, out_final, small_final,
    ) = pl.pallas_call(
        block_kernel,
        out_shape=[jax.ShapeDtypeStruct((256, 1024), BF16)] * 2
        + [
            jax.ShapeDtypeStruct(shape, F32)
            for shape in ((16, 2304), (16, 2304), (36, 1024), (3, 16, 512), (8, 1024), (8, 1024))
        ],
        in_specs=[vmem, vmem, far, vmem, far, vmem, far, far, far, vmem],
        out_specs=[vmem] * 8,
        scratch_shapes=scratch,
        compiler_params=pltpu.CompilerParams(
            collective_id=0, has_side_effects=True, vmem_limit_bytes=62 * 2**20
        ),
        name="block",
    )(
        hidden_in, norm1_gain.reshape(1, 1024), in_weight.transpose(1, 0, 2), conv_weight.T, out_weight,
        norm2_gain.reshape(1, 1024), gate_weight, up_weight, down_weight, cotangent.reshape(8, 32, 1024),
    )
    (
        block_out, input_grad, gate_final, up_final, down_final, in_final, out_final, gain1_final, gain2_final,
        conv_final,
    ) = pl.pallas_call(
        finish_kernel,
        out_shape=[jax.ShapeDtypeStruct((256, 1024), BF16)] * 2
        + [
            jax.ShapeDtypeStruct(shape, F32)
            for shape in (
                (16, 2304), (16, 2304), (36, 1024), (3, 16, 512), (8, 1024), (1, 16), (1, 16), (3, 8),
            )
        ],
        in_specs=[vmem] * 8,
        out_specs=[vmem] * 10,
        name="finish",
    )(block_out, input_grad, gate_final, up_final, down_final, in_final, out_final, small_final)
    return (
        block_out,
        input_grad,
        gain1_final.reshape(16),
        in_final.transpose(1, 0, 2),
        conv_final.T,
        out_final,
        gain2_final.reshape(16),
        gate_final,
        up_final,
        down_final,
    )


def solution(mesh):
    placed = (
        P("seq", None),
        P(),
        P(None, None, "head"),
        P("head", None),
        P("head", None),
        P(),
        P(None, "head"),
        P(None, "head"),
        P("head", None),
        P("seq", None),
    )
    return jax.shard_map(
        shards,
        mesh=mesh,
        in_specs=placed,
        out_specs=(
            P("seq", None),
            P("seq", None),
            P("seq"),
            P("seq", None, "head"),
            P(("head", "seq"), None),
            P(("head", "seq"), None),
            P("seq"),
            P("seq", "head"),
            P("seq", "head"),
            P(("head", "seq"), None),
        ),
        check_vma=False,
    )
```

```python
import jax
import jax.numpy as jnp
from jax import lax
from jax.experimental import pallas as pl
from jax.experimental.pallas import tpu as pltpu
from jax.sharding import PartitionSpec as P

EPS = 1e-05
MESH = pl.DeviceIdType.MESH
F32 = jnp.float32
BF16 = jnp.bfloat16
NT = (((1,), (1,)), ((), ()))
N_SEMS = 210
TILE = 768
CUTS = (0, 256, 896, 1536)


class Place:
    def __init__(self):
        self.seq = lax.axis_index("seq")
        self.head = lax.axis_index("head")
        self.coord = {
            "z": lax.div(self.seq, 16),
            "x": lax.rem(lax.div(self.seq, 4), 4),
            "y": lax.rem(self.seq, 4),
        }

        self.blocks = {
            axis: [self.coord[axis]] + [lax.rem(self.coord[axis] + shift, 4) for shift in (1, 2, 3)]
            for axis in "zxy"
        }
        self.peers = {}
        for axis in "zxy":
            for shift in (1, 2, 3):
                moved = dict(self.coord)
                moved[axis] = self.blocks[axis][shift]
                self.peers[axis, shift] = ((moved["z"] * 4 + moved["x"]) * 4 + moved["y"], self.head)
        self.along = {
            shift: (lax.rem(self.seq + 64 + shift, 64), self.head) for shift in (1, -1)
        }

    def peer(self, axis, shift):
        return self.peers[axis, shift]

    def diagonal(self, first, shift, second, other):
        moved = dict(self.coord)
        moved[first] = self.blocks[first][shift]
        moved[second] = self.blocks[second][other]
        return ((moved["z"] * 4 + moved["x"]) * 4 + moved["y"], self.head)

    def sibling(self):
        return (self.seq, 1 - self.head)


class Links:
    def __init__(self, send_sem, recv_sem):
        self.send_sem = send_sem
        self.recv_sem = recv_sem
        self.used = 0
        self.open = []

    def plan(self, src, dst, device):
        copy = pltpu.make_async_remote_copy(
            src_ref=src,
            dst_ref=dst,
            send_sem=self.send_sem.at[self.used],
            recv_sem=self.recv_sem.at[self.used],
            device_id=device,
            device_id_type=MESH,
        )
        self.used += 1
        return copy

    def send(self, src, dst, device):
        copy = self.plan(src, dst, device)
        copy.start()
        self.open.append(copy)
        return copy

    def close(self):
        for copy in self.open:
            copy.wait_send()
        self.open = []


class Ring:
    def __init__(self, place, links, axis, view, first, second):
        self.place, self.links, self.axis, self.view = place, links, axis, view
        self.first, self.second = first, second
        self.me = place.coord[axis]

    def block(self, shift):
        return self.place.blocks[self.axis][shift]

    def start(self):
        right, left = self.place.peer(self.axis, 1), self.place.peer(self.axis, 3)
        send = self.links.send
        self.far = [
            send(self.view(self.block(2), 0), self.first.at[0], right),
            send(self.view(self.block(2), 1), self.first.at[1], left),
        ]
        self.near = [
            send(self.view(self.block(1), 1), self.second.at[0, 1], right),
            send(self.view(self.block(3), 0), self.second.at[1, 0], left),
        ]

    def pass_on(self):
        right, left = self.place.peer(self.axis, 1), self.place.peer(self.axis, 3)
        for half, shift, device in ((0, 1, right), (1, 3, left)):
            self.far[half].wait_recv()
            own = self.view(self.block(shift), half)
            own[...] = (own[...].astype(F32) + self.first[half].astype(F32)).astype(BF16)
            self.near.append(self.links.send(own, self.second.at[half, half], device))

    def total(self, half):
        if half == 0:
            for copy in self.near:
                copy.wait_recv()
        own = self.view(self.block(0), half)[...].astype(F32)
        return own + self.second[0, half].astype(F32) + self.second[1, half].astype(F32)


class Plane:
    def __init__(self, place, links, axes, src, got):
        first, second = axes
        here = (place.coord[first], place.coord[second])
        self.copies = []
        for shift in (2, 1, 3, 0):
            for other in (2, 1, 3, 0):
                if shift or other:
                    there = src.at[place.blocks[first][shift], place.blocks[second][other]]
                    device = place.diagonal(first, shift, second, other)
                    self.copies.append(links.send(there, got.at[here[0], here[1]], device))
        got[here[0], here[1]] = src[here[0], here[1]]

    def wait(self):
        for copy in self.copies:
            copy.wait_recv()


def halves_of(ref, axis_dim, half_dim):
    extent = ref.shape[half_dim] // 2

    def view(block, half):
        index = [slice(None)] * len(ref.shape)
        index[half_dim] = pl.ds(half * extent, extent)
        index[axis_dim] = block
        return ref.at[tuple(index)]

    return view


def in_rows(extent, step, body, carry=0):
    def one(i, carry):
        return body(pl.multiple_of(i * step, step), carry)

    return lax.fori_loop(0, extent // step, one, carry)


def mean_square(values):
    return jnp.mean(values * values, axis=-1, keepdims=True)


def block_kernel(
    hin, gain1, w_in, w_conv, w_out, gain2, w_gate, w_up, w_down, cot,
    block_out, input_grad, gate_out, up_out, down_out, in_out, out_out, small_out,
    win, wout, n1, n1t, n2, n2t, hidt, gatet, upt, proj, gbuf, cv, mixed, mixedt, mid, mlow, cgbuf, mxg, pg,
    small, xb, xf, xn, xh,
    n2x, n2y, cotz, gx, uy, hz,
    g1a, g1b, g3, u1a, u1b, u3, d1a, d1b, d3,
    ia1, ia2, ib1, ib2, i3, ja1, ja2, jb1, jb2, j3, ka1, ka2, kb1, kb2, k3, oa1, oa2, ob1, ob2, o3,
    sm1, sm2,
    send_sem, recv_sem, load_sem,
):
    place = Place()
    links = Links(send_sem, recv_sem)
    head = place.head
    barrier = pltpu.get_barrier_semaphore()
    peers = [place.peer(axis, shift) for axis in "zxy" for shift in (1, 2, 3)]
    for first, second in ("zx", "xy"):
        peers += [place.diagonal(first, i, second, j) for i in (1, 2, 3) for j in (1, 2, 3)]
    peers += [place.sibling(), place.along[1], place.along[-1]]
    carried = jnp.where(lax.rem(place.seq, 16) != 0, 1.0, 0.0).astype(F32)
    carried_on = jnp.where(lax.rem(place.seq, 16) != 15, 1.0, 0.0).astype(F32)
    gathered = {}
    traded = {}
    shared = {}

    for axis, src, dst in (("z", cot, cotz), ("x", n2t, n2x), ("y", n2t, n2y)):
        part = src.shape[0] // 2
        mine = pl.ds(part * head, part)
        for shift in (1, 3, 2) if axis == "z" else (1, 3):
            gathered[axis, shift] = links.plan(
                src.at[mine], dst.at[shift - 1, mine], place.peer(axis, shift)
            )
        if axis != "z":
            for shift, here in ((1, 2 * head), (3, 2 * head + 1)):
                gathered[axis, 2, shift] = links.plan(
                    dst.at[shift - 1, here], dst.at[1, here], place.peer(axis, shift)
                )

    def gather(axis):
        for shift in (1, 3, 2) if axis == "z" else (1, 3):
            gathered[axis, shift].start()

    def relay(axis):
        for shift in (1, 3):
            gathered[axis, shift].wait_recv()
            gathered[axis, 2, shift].start()

    for axis, src, dst in (("z", hidt, hz), ("x", gatet, gx), ("y", upt, uy)):
        for shift in (1, 3, 2):
            rows = pl.ds(pl.multiple_of(place.blocks[axis][shift] * 576, 576), 576)
            traded[axis, shift] = links.plan(src.at[rows], dst.at[shift - 1], place.peer(axis, shift))
    back_link = links.plan(xn.at[0], xn.at[1], place.sibling())
    ffn_link = links.plan(xf.at[0], xf.at[1], place.sibling())

    def share(axis, dst):
        for shift in (1, 3, 2):
            if axis == "z":
                gathered[axis, shift].wait_recv()
            elif shift == 2:
                gathered[axis, 2, 1].wait_recv()
                gathered[axis, 2, 3].wait_recv()
            part = dst.shape[1] // 2
            here = dst.at[shift - 1, pl.ds(part * head, part)]
            shared[axis, shift] = links.send(here, here, place.sibling())

    taps = w_conv[...]

    def shifted_gated(r):
        window = gbuf[pl.ds(r, 48), :].astype(F32)
        return [pltpu.roll(window, 2, 0)[16:], pltpu.roll(window, 1, 0)[16:], window[16:]]

    def forward(wg, wu, wd, pre_g, pre_u, grad_h, hid_s, gg_s, ug_s, n2g_acc):
        loads = []
        for src, dst in (
            (w_in.at[0], win.at[0]), (w_in.at[1], win.at[1]), (w_in.at[2], win.at[2]),
            (w_out, wout), (w_down, wd), (w_gate, wg), (w_up, wu),
        ):
            loads.append(pltpu.make_async_copy(src, dst, load_sem.at[len(loads)]))
        for copy in loads[:4]:
            copy.start()
        for device in peers:
            pl.semaphore_signal(barrier, inc=1, device_id=device, device_id_type=MESH)

        def norm_one(r, carry):
            x = hin[pl.ds(r, 32), :].astype(F32)
            n1[pl.ds(r, 32), :] = (x * lax.rsqrt(mean_square(x) + EPS) * gain1[...]).astype(BF16)
            return carry

        in_rows(256, 32, norm_one)
        pl.semaphore_wait(barrier, len(peers))
        gather("z")
        for part in (0, 2, 1):
            loads[part].wait()
            if part == 2:
                for copy in loads[4:]:
                    copy.start()
            proj[part] = jnp.dot(n1[...], win[part], preferred_element_type=F32)
            if part == 2:
                def gate_rows(r, carry):
                    here = pl.ds(r, 32)
                    gbuf[pl.ds(r + 16, 32), :] = (proj[0, here, :] * proj[2, here, :]).astype(BF16)
                    return carry

                in_rows(256, 32, gate_rows)
                edge = links.send(gbuf.at[pl.ds(256, 16)], gbuf.at[pl.ds(0, 16)], place.along[1])
        for i in range(4):
            n1t[i] = n1[:, 256 * i:256 * i + 256].T
        loads[3].wait()
        loads[4].wait()

        def hidden_grad(tile):
            part = wd[tile * TILE:tile * TILE + TILE, :]
            grad_h[tile] = lax.dot_general(
                cot[...].reshape(256, 1024), part, NT, preferred_element_type=F32
            )

        hidden_grad(0)
        hidden_grad(1)
        edge.wait_recv()
        gbuf[pl.ds(0, 16), :] = (gbuf[pl.ds(0, 16), :].astype(F32) * carried).astype(BF16)

        def mix_rows(r, carry):
            here = pl.ds(r, 32)
            old, last, now = shifted_gated(r)
            value = taps[0:1] * old + taps[1:2] * last + taps[2:3] * now
            cv[here, :] = value
            mixed[here, :] = (proj[1, here, :] * value).astype(BF16)
            return carry

        in_rows(256, 32, mix_rows)
        branch = []
        for half in range(2):
            here = pl.ds(128 * half, 128)
            xb[0, here, :] = jnp.dot(mixed[here, :], wout[...], preferred_element_type=F32).astype(BF16)
            branch.append(links.send(xb.at[0, here], xb.at[1, here], place.sibling()))
        for i in range(4):
            mixedt[i] = mixed[:, 128 * i:128 * i + 128].T

        hidden_grad(2)

        def norm_two(r, carry):
            here = pl.ds(r, 32)
            middle = hin[here, :].astype(F32) + (xb[0, here, :].astype(F32) + xb[1, here, :].astype(F32))
            mid[here, :] = middle
            n2[here, :] = (middle * lax.rsqrt(mean_square(middle) + EPS) * gain2[...]).astype(BF16)
            return carry

        for half in range(2):
            branch[half].wait_recv()
            in_rows(128, 32, lambda r, carry: norm_two(r + 128 * half, carry))
        for i in range(4):
            n2t[i] = n2[:, 256 * i:256 * i + 256].T
        gather("x")
        gather("y")
        for copy in loads[5:]:
            copy.wait()
        for t in range(0, 2304, TILE):
            cut = slice(t, t + TILE)
            pre_g[...] = jnp.dot(n2[...], wg[:, cut], preferred_element_type=F32)
            pre_u[...] = jnp.dot(n2[...], wu[:, cut], preferred_element_type=F32)
            if t + TILE == 2304:
                relay("x")
                relay("y")

            def act_rows(r, carry, t=t):
                here = pl.ds(r, 32)
                gate, up, grad = pre_g[here, :], pre_u[here, :], grad_h[t // TILE, here, :]
                sig = jax.nn.sigmoid(gate)
                act = gate * sig
                hid_s[here, t:t + TILE] = (act * up).astype(BF16)
                gg_s[here, :] = (grad * up * (sig * (1.0 + gate * (1.0 - sig)))).astype(BF16)
                ug_s[here, :] = (grad * act).astype(BF16)
                return carry

            in_rows(256, 32, act_rows)
            hidt[cut, :] = hid_s[:, cut].T
            gatet[cut, :] = gg_s[...].T
            upt[cut, :] = ug_s[...].T
            last = t + TILE == 2304
            if last:
                for copy in traded.values():
                    copy.start()
            back = lax.dot_general(gg_s[...], wg[:, cut], NT, preferred_element_type=F32)
            back += lax.dot_general(ug_s[...], wu[:, cut], NT, preferred_element_type=F32)
            if t > 0:
                back += n2g_acc[...]
            if last:
                xn[0] = back.astype(BF16)
            else:
                n2g_acc[...] = back
        back_link.start()
        xf[0] = jnp.dot(hid_s[...], wd[...], preferred_element_type=F32).astype(BF16)
        ffn_link.start()
        links.close()

    v = lambda *shape: pltpu.VMEM(shape, BF16)
    f = lambda *shape: pltpu.VMEM(shape, F32)
    pl.run_scoped(
        forward, v(1024, 2304), v(1024, 2304), v(2304, 1024),
        f(256, TILE), f(256, TILE), f(3, 256, TILE), v(256, 2304), v(256, TILE), v(256, TILE),
        f(256, 1024),
    )

    def backward(g1, g2, u1, u2, d1, dt, d2, ia, ib, ic, ja, jb, jc, ka, kb, kc, oa, ob, oc):
        share("z", cotz)
        back_link.wait_recv()
        ffn_link.wait_recv()
        small[...] = jnp.zeros((8, 1024), F32)

        def norm_two_back(i, total):
            here = pl.ds(pl.multiple_of(i * 32, 32), 32)
            grad = xn[0, here, :].astype(F32) + xn[1, here, :].astype(F32)
            middle = mid[here, :]
            ffn = xf[0, here, :].astype(F32) + xf[1, here, :].astype(F32)
            block_out[here, :] = (middle + ffn).astype(BF16)
            scale = lax.rsqrt(mean_square(middle) + EPS)
            unit = middle * scale
            total += jnp.sum((grad * unit).reshape(4, 8, 1024), axis=0)
            inner = grad * gain2[...]
            inner = scale * (inner - unit * jnp.mean(inner * unit, axis=-1, keepdims=True))
            middle = cot[i].astype(F32) + inner
            mid[here, :] = middle
            mlow[here, :] = middle.astype(BF16)
            return total

        total = lax.fori_loop(0, 8, norm_two_back, jnp.zeros((8, 1024), F32))
        small[1:2, :] = jnp.sum(total, axis=0, keepdims=True)
        def out_tile(i, carry):
            res = jnp.dot(mixedt[i], mlow[...], preferred_element_type=F32)
            oa[i] = res.astype(BF16).reshape(8, 16, 1024)
            return carry

        lax.fori_loop(0, 4, out_tile, 0)
        out_ring = Ring(place, links, "z", halves_of(oa, 0, 1), oa1, oa2)
        out_ring.start()
        mxg[...] = lax.dot_general(mlow[...], wout[...], NT, preferred_element_type=F32)

        def conv_back(r, totals):
            here = pl.ds(r, 32)
            grad = mxg[here, :]
            back = grad * proj[1, here, :]
            cgbuf[here, :] = back
            pg[here, 512:1024] = (grad * cv[here, :]).astype(BF16)
            return tuple(
                t + jnp.sum((back * g).reshape(4, 8, 512), axis=0) for t, g in zip(totals, shifted_gated(r))
            )

        totals = in_rows(256, 32, conv_back, (jnp.zeros((8, 512), F32),) * 3)
        edge = links.send(cgbuf.at[pl.ds(0, 8)], cgbuf.at[pl.ds(256, 8)], place.along[-1])
        for k in range(3):
            small[2 + k:3 + k, 0:512] = jnp.sum(totals[k], axis=0, keepdims=True)

        edge.wait_recv()
        cgbuf[pl.ds(256, 8), :] = cgbuf[pl.ds(256, 8), :] * carried_on

        def taps_back(r, carry):
            here = pl.ds(r, 32)
            window = cgbuf[pl.ds(r, 40), :]
            grad = (
                taps[2:3] * window[:32]
                + taps[1:2] * pltpu.roll(window, 39, 0)[:32]
                + taps[0:1] * pltpu.roll(window, 38, 0)[:32]
            )
            pg[here, 0:512] = (grad * proj[2, here, :]).astype(BF16)
            pg[here, 1024:1536] = (grad * proj[0, here, :]).astype(BF16)
            return carry

        in_rows(256, 32, taps_back)
        part = lax.dot_general(pg[:, 0:512], win[0], NT, preferred_element_type=F32)
        part += lax.dot_general(pg[:, 512:1024], win[1], NT, preferred_element_type=F32)
        part += lax.dot_general(pg[:, 1024:1536], win[2], NT, preferred_element_type=F32)
        xh[0] = part.astype(BF16)
        first_link = links.send(xh.at[0], xh.at[1], place.sibling())

        in_rings = [
            Ring(place, links, "z", lambda b, h: ia.at[b, pl.ds(2 * h, 2)], ia1, ia2),
            Ring(place, links, "x", lambda b, h: ja.at[pl.ds(2 * h, 2), b], ja1, ja2),
            Ring(place, links, "y", lambda b, h: ka.at[pl.ds(2 * h, 2), :, b], ka1, ka2),
        ]
        for part, own in enumerate((ia, ja, ka)):
            def in_tile(i, carry, own=own, left=CUTS[part], right=CUTS[part + 1]):
                res = jnp.dot(n1t[i], pg[:, left:right], preferred_element_type=F32)
                own[i] = res.astype(BF16).reshape(4, 4, 16, right - left)
                return carry

            lax.fori_loop(0, 4, in_tile, 0)
            in_rings[part].start()

        def ready(axis):
            for shift in (1, 3, 2):
                shared[axis, shift].wait_recv()
                traded[axis, shift].wait_recv()

        share("x", n2x)
        share("y", n2y)
        first_link.wait_recv()

        def norm_one_back(r, total):
            here = pl.ds(r, 32)
            grad = xh[0, here, :].astype(F32) + xh[1, here, :].astype(F32)
            x = hin[here, :].astype(F32)
            scale = lax.rsqrt(mean_square(x) + EPS)
            unit = x * scale
            total += jnp.sum((grad * unit).reshape(4, 8, 1024), axis=0)
            inner = grad * gain1[...]
            inner = scale * (inner - unit * jnp.mean(inner * unit, axis=-1, keepdims=True))
            input_grad[here, :] = (mid[here, :] + inner).astype(BF16)
            return total

        total = in_rows(256, 32, norm_one_back, jnp.zeros((8, 1024), F32))
        small[0:1, :] = jnp.sum(total, axis=0, keepdims=True)
        small_links = [links.send(small, sm1.at[0, shift - 1], place.peer("z", shift)) for shift in (1, 3, 2)]

        def wide(own_x, got_x, own_g, got_g, me, store):
            def tile(i, carry):
                own = own_g[pl.ds(pl.multiple_of(me * 576, 576), 576), :]
                res = lax.dot_general(own_x[i], own, NT, preferred_element_type=F32)
                for d in range(3):
                    res += lax.dot_general(got_x[d, i], got_g[d], NT, preferred_element_type=F32)
                store(i, res.astype(BF16))
                return carry

            lax.fori_loop(0, 4, tile, 0)

        ready("z")

        def down_tile(i, carry):
            own = hidt[pl.ds(pl.multiple_of(place.coord["z"] * 576 + i * 144, 144), 144), :]
            res = jnp.dot(own, cot[...].reshape(256, 1024), preferred_element_type=F32)
            for d in range(3):
                got = hz[d, pl.ds(pl.multiple_of(i * 144, 144), 144), :]
                res += jnp.dot(got, cotz[d].reshape(256, 1024), preferred_element_type=F32)
            d1[i] = res.astype(BF16).reshape(9, 16, 1024)
            return carry

        lax.fori_loop(0, 4, down_tile, 0)
        down_ring = Ring(place, links, "x", halves_of(d1, 0, 3), d1a, d1b)
        down_ring.start()

        for ring in in_rings:
            ring.pass_on()
        out_ring.pass_on()

        ready("x")

        def gate_store(i, res):
            g1[pl.ds(4 * i, 4)] = res.reshape(4, 4, 16, 576)

        wide(n2t, n2x, gatet, gx, place.coord["x"], gate_store)
        gate_ring = Ring(place, links, "y", halves_of(g1, 1, 0), g1a, g1b)
        gate_ring.start()

        ready("y")

        def up_store(i, res):
            u1[i] = res.reshape(16, 16, 576)

        wide(n2t, n2y, upt, uy, place.coord["y"], up_store)
        up_ring = Ring(place, links, "z", halves_of(u1, 0, 1), u1a, u1b)
        up_ring.start()

        for copy in small_links:
            copy.wait_recv()
        sm2[0] = small[...] + sm1[0, 0] + sm1[0, 1] + sm1[0, 2]
        small_links = [links.send(sm2.at[0], sm1.at[1, shift - 1], place.peer("x", shift)) for shift in (1, 3, 2)]
        down_ring.pass_on()

        gate_ring.pass_on()
        up_ring.pass_on()
        for ring, own in zip(in_rings, (ib, jb, kb)):
            for half in range(2):
                own[pl.ds(2 * half, 2)] = ring.total(half).astype(BF16)
        for half in range(2):
            res = out_ring.total(half).reshape(2, 4, 8, 1024)
            res = jnp.concatenate([res[..., :512], res[..., 512:]], axis=2)
            ob[pl.ds(2 * half, 2)] = res.astype(BF16)
        in_rings = [
            Ring(place, links, "x", halves_of(ib, 0, 1), ib1, ib2),
            Ring(place, links, "y", halves_of(jb, 1, 0), jb1, jb2),
            Ring(place, links, "z", halves_of(kb, 0, 1), kb1, kb2),
            Ring(place, links, "x", halves_of(ob, 0, 1), ob1, ob2),
        ]
        for ring in in_rings:
            ring.start()
        for copy in small_links:
            copy.wait_recv()
        sm2[1] = sm2[0] + sm1[1, 0] + sm1[1, 1] + sm1[1, 2]
        small_links = [links.send(sm2.at[1], sm1.at[2, shift - 1], place.peer("y", shift)) for shift in (1, 3, 2)]

        for ring in in_rings:
            ring.pass_on()
        dt[pl.ds(144, 16), :] = jnp.zeros((16, 1024), F32)
        for half in range(2):
            dt[pl.ds(0, 144), half * 512:(half + 1) * 512] = down_ring.total(half).reshape(144, 512)
        for y in range(4):
            d2[y] = dt[pl.ds(36 * y, 48), :].astype(BF16)
        down_links = [
            links.send(d2.at[place.blocks["y"][shift]], d3.at[shift - 1], place.peer("y", shift))
            for shift in (2, 1, 3)
        ]
        for half in range(2):
            g2[pl.ds(2 * half, 2)] = gate_ring.total(half).astype(BF16).reshape(2, 4, 16, 576)
        gate_plane = Plane(place, links, "zx", g2, g3)
        in_links = []
        lines = (("y", ic, i3), ("z", jc, j3), ("x", kc, k3), ("y", oc, o3))
        for ring, (axis, own, got) in zip(in_rings, lines):
            for half in range(2):
                own[pl.ds(2 * half, 2)] = ring.total(half).astype(BF16)
            for shift in (2, 1, 3):
                there = own.at[place.blocks[axis][shift]]
                in_links.append(links.send(there, got.at[shift - 1], place.peer(axis, shift)))
        for half in range(2):
            u2[pl.ds(2 * half, 2)] = up_ring.total(half).astype(BF16).reshape(2, 4, 16, 576)
        up_plane = Plane(place, links, "xy", u2, u3)

        for copy in small_links:
            copy.wait_recv()
        small_out[...] = sm2[1] + sm1[2, 0] + sm1[2, 1] + sm1[2, 2]
        for copy in down_links:
            copy.wait_recv()
        res = d2[place.coord["y"]].astype(F32)
        for d in range(3):
            res += d3[d].astype(F32)
        down_out[...] = res[:36]
        gate_plane.wait()
        gate_out[...] = jnp.concatenate([jnp.sum(g3[:, x].astype(F32), axis=0) for x in range(4)], axis=1)
        up_plane.wait()
        up_out[...] = jnp.concatenate([jnp.sum(u3[:, y].astype(F32), axis=0) for y in range(4)], axis=1)
        for copy in in_links:
            copy.wait_recv()
        sums = []
        for axis, own, got in lines:
            res = own[place.coord[axis]].astype(F32)
            for d in range(3):
                res += got[d].astype(F32)
            sums.append(res)
        res = jnp.concatenate(sums[:3], axis=1)
        for part in range(3):
            in_out[part] = res[:, 512 * part:512 * part + 512]
        out_out[:, 0:512] = sums[3][:8]
        out_out[:, 512:1024] = sums[3][8:]
        links.close()
        for copy in (*gathered.values(), *traded.values(), back_link, ffn_link):
            copy.wait_send()

    pl.run_scoped(
        backward,
        v(16, 4, 16, 576), v(4, 4, 16, 576), v(4, 16, 16, 576), v(4, 4, 16, 576),
        v(4, 9, 16, 1024), f(160, 1024), v(4, 48, 1024),
        *[v(*([4] * dims), 16, width) for width in (256, 640, 640) for dims in (3, 2, 1)],
        v(4, 8, 16, 1024), v(4, 4, 16, 512), v(4, 16, 512),
    )


def finish_kernel(
    block_in, grad_in, gate_in, up_in, down_in, in_in, out_in, small_in,
    block_out, input_grad, gate_out, up_out, down_out, in_out, out_out, gain1_out, gain2_out, conv_out,
):
    place = lax.axis_index("seq")
    for src, dst in (
        (block_in, block_out), (grad_in, input_grad), (gate_in, gate_out), (up_in, up_out),
        (down_in, down_out), (in_in, in_out), (out_in, out_out),
    ):
        dst[...] = src[...]
    gains = pltpu.roll(small_in[...], 1024 - 16 * place, 1)
    gain1_out[...] = gains[0:1, 0:16]
    gain2_out[...] = gains[1:2, 0:16]
    taps = pltpu.roll(small_in[...], 1024 - 8 * place, 1)
    conv_out[...] = taps[2:5, 0:8]


def shards(
    hidden_in, norm1_gain, in_weight, conv_weight, out_weight, norm2_gain, gate_weight, up_weight, down_weight,
    cotangent,
):
    v = lambda *shape: pltpu.VMEM(shape, BF16)
    f = lambda *shape: pltpu.VMEM(shape, F32)

    def ring(*half):
        return [v(2, *half), v(2, 2, *half)]

    scratch = [
        v(3, 1024, 512), v(512, 1024), v(256, 1024), v(4, 256, 256), v(256, 1024), v(4, 256, 256),
        v(2304, 256), v(2304, 256), v(2304, 256), f(3, 256, 512), v(272, 512), f(256, 512), v(256, 512),
        v(4, 128, 256), f(256, 1024), v(256, 1024), f(264, 512), f(256, 512), v(256, 1536), f(8, 1024),
        *[v(2, 256, 1024)] * 4,
        v(3, 4, 256, 256), v(3, 4, 256, 256), v(3, 8, 32, 1024),
        v(3, 576, 256), v(3, 576, 256), v(3, 576, 256),
        *ring(8, 16, 576), v(4, 4, 16, 576), *ring(8, 16, 576), v(4, 4, 16, 576), *ring(9, 16, 512), v(3, 48, 1024),
        *[
            buffer
            for width in (256, 640, 640)
            for buffer in (*ring(2, 4, 16, width), *ring(2, 16, width), v(3, 16, width))
        ],
        *ring(4, 16, 1024), *ring(2, 16, 512), v(3, 16, 512),
        f(3, 3, 8, 1024), f(2, 8, 1024),
        pltpu.SemaphoreType.DMA((N_SEMS,)), pltpu.SemaphoreType.DMA((N_SEMS,)), pltpu.SemaphoreType.DMA((7,)),
    ]
    vmem = pl.BlockSpec(memory_space=pltpu.VMEM)
    far = pl.BlockSpec(memory_space=pl.ANY)
    (
        block_out, input_grad, gate_final, up_final, down_final, in_final, out_final, small_final,
    ) = pl.pallas_call(
        block_kernel,
        out_shape=[jax.ShapeDtypeStruct((256, 1024), BF16)] * 2
        + [
            jax.ShapeDtypeStruct(shape, F32)
            for shape in ((16, 2304), (16, 2304), (36, 1024), (3, 16, 512), (8, 1024), (8, 1024))
        ],
        in_specs=[vmem, vmem, far, vmem, far, vmem, far, far, far, vmem],
        out_specs=[vmem] * 8,
        scratch_shapes=scratch,
        compiler_params=pltpu.CompilerParams(
            collective_id=0, has_side_effects=True, vmem_limit_bytes=62 * 2**20
        ),
        name="block",
    )(
        hidden_in, norm1_gain.reshape(1, 1024), in_weight.transpose(1, 0, 2), conv_weight.T, out_weight,
        norm2_gain.reshape(1, 1024), gate_weight, up_weight, down_weight, cotangent.reshape(8, 32, 1024),
    )
    (
        block_out, input_grad, gate_final, up_final, down_final, in_final, out_final, gain1_final, gain2_final,
        conv_final,
    ) = pl.pallas_call(
        finish_kernel,
        out_shape=[jax.ShapeDtypeStruct((256, 1024), BF16)] * 2
        + [
            jax.ShapeDtypeStruct(shape, F32)
            for shape in (
                (16, 2304), (16, 2304), (36, 1024), (3, 16, 512), (8, 1024), (1, 16), (1, 16), (3, 8),
            )
        ],
        in_specs=[vmem] * 8,
        out_specs=[vmem] * 10,
        name="finish",
    )(block_out, input_grad, gate_final, up_final, down_final, in_final, out_final, small_final)
    return (
        block_out,
        input_grad,
        gain1_final.reshape(16),
        in_final.transpose(1, 0, 2),
        conv_final.T,
        out_final,
        gain2_final.reshape(16),
        gate_final,
        up_final,
        down_final,
    )


def solution(mesh):
    placed = (
        P("seq", None),
        P(),
        P(None, None, "head"),
        P("head", None),
        P("head", None),
        P(),
        P(None, "head"),
        P(None, "head"),
        P("head", None),
        P("seq", None),
    )
    return jax.shard_map(
        shards,
        mesh=mesh,
        in_specs=placed,
        out_specs=(
            P("seq", None),
            P("seq", None),
            P("seq"),
            P("seq", None, "head"),
            P(("head", "seq"), None),
            P(("head", "seq"), None),
            P("seq"),
            P("seq", "head"),
            P("seq", "head"),
            P(("head", "seq"), None),
        ),
        check_vma=False,
    )
```
